256 devices in a mesh: ctx: 64 (over z, y, x_hi), head: 4 (over x_lo, core).
Axes of the slice: x: 4 (x_hi: 2, x_lo: 2; x = x_hi * 2 + x_lo), y: 4, z: 8, core: 2. Of those that a mesh axis runs over, the one named last changes fastest.
Arguments:
- queries: bfloat16 [16384, 4096], P('ctx', 'head'), may hold values from -6 to 6
- keys: bfloat16 [16384, 512], P('ctx', 'head'), may hold values from -6 to 6
- values: bfloat16 [16384, 512], P('ctx', 'head'), may hold values from -24 to 24
- w_in: bfloat16 [4096, 16384], P('head', 'ctx'), may hold values from -0.09375 to 0.09375
- w_out: bfloat16 [16384, 2], P('ctx'), may hold values from -0.09375 to 0.09375
- step_pos: int32 [256], replicated, may hold values from 0 to 16383, as said below
- step_attr: int32 [256], replicated, may hold values from 0 to 3
Outputs:
- attn_out: bfloat16 [16384, 4096], P('ctx', 'head')
- step_logits: float32 [256, 2], replicated
The draws below stay inside these ranges and needn't reach their ends.
Inputs may be any that keep to these rules, and one draw needn't show every extreme that they name: `step_pos`: strictly increasing; the last token, 16383, ends the final step. The 256 tokens of any one index of ctx hold at most 8 step ends, and some index holds exactly 8.
All inputs are finite; a program needn't handle non-finite values.
Results may differ from the reference program's by a relative error of at most 0.02.
Values may be sent and summed in bfloat16 or wider, within the bound.
A program may use at most 64 MiB of HBM per device.

```python
import math
import jax
import jax.numpy as jnp
from jax import lax

QH = 32
KH = 4
HD = 128
HID = 4096
ATTRS = 4
NOUT = 2
TOK_DEV = 256
STEPS_DEV = 4
SEQ = 16384
STEPS = 256
FEAT = 4096
N_CTX = 64


def draw_queries(key, part):
    key = jax.random.fold_in(key, 3)
    full = jnp.clip(jax.random.normal(key, (SEQ, QH, HD), jnp.float32) * 1.6, -6.0, 6.0)
    return full.reshape(SEQ, QH * HD).astype(jnp.bfloat16)


def draw_keys(key, part):
    key = jax.random.fold_in(key, 4)
    full = jnp.clip(jax.random.normal(key, (SEQ, KH, HD), jnp.float32) * 1.6, -6.0, 6.0)
    return full.reshape(SEQ, KH * HD).astype(jnp.bfloat16)


def draw_values(key, part):
    key = jax.random.fold_in(key, 5)
    noise_key, scale_key = jax.random.split(key)
    noise = jnp.clip(jax.random.normal(noise_key, (SEQ, KH, HD), jnp.float32), -4.0, 4.0)
    rise = 3.0
    spread = 10.0
    channel = jnp.exp(jax.random.uniform(scale_key, (KH, HD), jnp.float32) * jnp.log(spread)) / jnp.sqrt(spread)
    ladder = jnp.power(rise, jnp.arange(KH, dtype=jnp.float32) / (KH - 1)) / jnp.sqrt(rise)
    full = noise * channel[None, :, :] * ladder[None, :, None]
    return full.reshape(SEQ, KH * HD).astype(jnp.bfloat16)


def draw_step_pos(key, part):
    key = jax.random.fold_in(key, 7)
    order_key, pick_key, split_key, offset_key = jax.random.split(key, 4)
    limit = 2 * STEPS_DEV
    half_count = N_CTX // 2
    last_device = N_CTX - 1
    order = jax.random.permutation(order_key, N_CTX)
    share = jax.random.randint(split_key, (half_count,), 0, limit + 1)
    chosen = jax.random.randint(pick_key, (), 0, half_count)
    share = jnp.where(jnp.arange(half_count) == chosen, limit, share)
    counts = jnp.zeros((N_CTX,), jnp.int32).at[order[0::2]].set(share).at[order[1::2]].set(limit - share)
    place = jnp.argsort(order)
    partner = order[place[last_device] ^ 1]
    swapped = counts.at[last_device].set(counts[partner]).at[partner].set(counts[last_device])
    counts = jnp.where(counts[last_device] == 0, swapped, counts)
    device_keys = jax.random.split(offset_key, N_CTX)
    drawn = jax.vmap(lambda single: jax.random.permutation(single, TOK_DEV)[:limit])(device_keys)
    ending = jax.random.permutation(jax.random.fold_in(offset_key, 11), TOK_DEV - 1)[:limit - 1]
    closing = jnp.concatenate([jnp.full((1,), TOK_DEV - 1, jnp.int32), ending.astype(jnp.int32)])
    device_ids = jnp.arange(N_CTX)
    offsets = jnp.where((device_ids == last_device)[:, None], closing[None, :], drawn.astype(jnp.int32))
    valid = jnp.arange(limit)[None, :] < counts[:, None]
    spots = jnp.where(valid, device_ids[:, None] * TOK_DEV + offsets, 2 * SEQ)
    return jnp.sort(spots.reshape(-1))[:STEPS].astype(jnp.int32)


def plant(drawn, rng, smallest, high):
    index_at = [jax.random.randint(jax.random.fold_in(rng, axis), (), 0, length) for axis, length in enumerate(drawn.shape)]
    longest = drawn.shape.index(max(drawn.shape))
    beside = index_at[:longest] + [(index_at[longest] + 1) % drawn.shape[longest]] + index_at[longest + 1:]
    return drawn.at[tuple(index_at)].set(smallest).at[tuple(beside)].set(high)


def shard_levels(own_key, shape, shards, least, largest):
    def one(axis_at, blocks):
        heights = jax.random.uniform(jax.random.fold_in(jax.random.fold_in(own_key, 6), axis_at), (blocks,), jnp.float32, least / len(shards), largest / len(shards))
        return jnp.repeat(jnp.exp(heights), shape[axis_at] // blocks).reshape((-1,) + (1,) * (len(shape) - axis_at - 1))

    factor_of = one(*shards[0])
    for cut in shards[1:]:
        factor_of = factor_of * one(*cut)
    return factor_of


def normal_values(stream_key, shape, scale, reach, cuts=(), kind=jnp.bfloat16):
    array = scale * jax.random.normal(stream_key, shape, jnp.float32)
    if cuts:
        array = array * shard_levels(stream_key, shape, cuts, -0.22, 0.18)
    return jnp.clip(array, -reach, reach).astype(kind)


def setup_inputs(seed: int = 0) -> dict:
    key_of = jax.random.split(jax.random.key(seed), 8)
    return {
        "queries": draw_queries(jax.random.fold_in(key_of[7], 71), 0),
        "keys": draw_keys(jax.random.fold_in(key_of[7], 71), 0),
        "values": draw_values(jax.random.fold_in(key_of[7], 71), 0),
        "w_in": normal_values(key_of[3], (FEAT, ATTRS * HID), FEAT ** -0.5, 0.09375, ((0, 4), (1, 64))),
        "w_out": normal_values(key_of[4], (ATTRS * HID, NOUT), HID ** -0.5, 0.09375, ((0, 64),)),
        "step_pos": draw_step_pos(jax.random.fold_in(key_of[7], 71), 0),
        "step_attr": plant(jax.random.randint(key_of[6], (STEPS,), 0, ATTRS), jax.random.fold_in(key_of[6], 1), 0, ATTRS - 1).astype(jnp.int32),
    }


def attend_reference(queries, keys, values):
    seq = queries.shape[0]
    group = QH // KH
    grouped = queries.reshape(seq, KH, group, HD)
    keys_three = keys.reshape(seq, KH, HD)
    values_three = values.reshape(seq, KH, HD)
    block = math.gcd(seq, 512)
    blocks = seq // block
    key_pos = jnp.arange(seq, dtype=jnp.int32)
    zero_index = jnp.zeros((), jnp.int32)

    def one_block(index):
        head_index = (index // blocks).astype(jnp.int32)
        begin = (index % blocks * block).astype(jnp.int32)
        query_part = lax.dynamic_slice(grouped, (begin, head_index, zero_index, zero_index), (block, 1, group, HD))[:, 0]
        key_head = lax.dynamic_index_in_dim(keys_three, head_index, 1, keepdims=False)
        value_head = lax.dynamic_index_in_dim(values_three, head_index, 1, keepdims=False)
        query_pos = begin + jnp.arange(block, dtype=jnp.int32)
        scores = jnp.einsum('qgd,kd->gqk', query_part.astype(jnp.float32), key_head.astype(jnp.float32)) * HD ** (-0.5)
        visible = key_pos[None, None, :] <= query_pos[None, :, None]
        row_top = lax.optimization_barrier(jnp.max(jnp.where(visible, scores, -1e+30), axis=-1))
        weights = jnp.where(visible, jnp.exp(scores - row_top[..., None]), 0.0)
        total = lax.optimization_barrier(jnp.sum(weights, axis=-1))
        rounded = weights.astype(jnp.bfloat16)
        mixed = jnp.einsum('gqk,kd->qgd', rounded.astype(jnp.float32), value_head.astype(jnp.float32))
        mixed = mixed / jnp.transpose(total)[:, :, None]
        return mixed.astype(jnp.bfloat16)
    parts = lax.map(one_block, jnp.arange(KH * blocks, dtype=jnp.int32))
    parts = parts.reshape(KH, blocks, block, group, HD).transpose(1, 2, 0, 3, 4)
    return parts.reshape(seq, KH * group * HD)

def reference(queries, keys, values, w_in, w_out, step_pos, step_attr):
    attn_out = attend_reference(queries, keys, values)
    features = jnp.take(attn_out, step_pos, axis=0)
    squares = lax.optimization_barrier(jnp.sum(jnp.square(features.astype(jnp.float32)), axis=1))
    factor = lax.rsqrt(squares / FEAT + 1e-06)
    pre = jnp.dot(features, w_in, preferred_element_type=jnp.float32) * factor[:, None]
    column_attr = jnp.arange(ATTRS * HID, dtype=jnp.int32) // HID
    keep = column_attr[None, :] == step_attr[:, None]
    hidden = jnp.where(keep, jax.nn.relu(pre), 0.0).astype(jnp.bfloat16)
    step_logits = jnp.dot(hidden, w_out, preferred_element_type=jnp.float32)
    return (attn_out, step_logits)
```

```python
import functools
import math

import jax
import jax.numpy as jnp
from jax import lax
from jax.experimental import pallas as pl
from jax.experimental.pallas import tpu as pltpu
from jax.sharding import PartitionSpec as P

HD = 128
GROUP = 8
ROWS = 256
HID = 4096
CAP = 8
FEAT = 4096
NORM_EPS = 1e-06
SCALE = HD ** -0.5 * math.log2(math.e)
HIDE = -1e30
MESH = pl.DeviceIdType.MESH
F32 = jnp.float32
BF16 = jnp.bfloat16

CHUNKS = (
    ((0, 0), (1, 0), (-1, 0), (0, 1)),
    ((0, -1), (2, 0), (-2, 0), (1, 1)),
    ((1, -1), (-1, 1), (-1, -1), (3, 0)),
    ((-3, 0), (2, 1), (2, -1), (-2, 1)),
    ((-2, -1), (4, 0), (3, 1), (3, -1)),
    ((-3, 1), (-3, -1), (4, 1), (4, -1)),
    ((0, 2), (1, 2), (-1, 2), (2, 2)),
    ((-2, 2), (3, 2), (-3, 2), (4, 2)),
)
PLACE = {spot: (n, j) for n, chunk in enumerate(CHUNKS) for j, spot in enumerate(chunk)}
DZ_ORDER = (0, 1, -1, 2, -2, 3, -3, 4)
TILES = GROUP
NCHUNK = len(CHUNKS)


def coords():
    ctx = lax.axis_index("ctx")
    head = lax.axis_index("head")
    return ctx // 8, (ctx // 2) % 4, ctx % 2, head // 2, head % 2


def device(z, y, x_hi, x_lo, core):
    return ((z * 4 + y) * 2 + x_hi, x_lo * 2 + core)


def attention_kernel(
    q_ref, k_ref, v_ref, o_ref,
    stage, kv, q_raw, q_t, acc, top, scores, tops, o_role, bias,
    swap_s, swap_r, z_s, z_r, y_s, y_r, sib_s, sib_r,
):
    z, y, x_hi, x_lo, core = coords()
    stays = x_hi == core
    swap_dev = device(z, y, core, x_lo, x_hi)
    sib_dev = device(z, y, x_hi, x_lo, 1 - core)
    z_dev = {1: device((z + 1) % 8, y, x_hi, x_lo, core), -1: device((z + 7) % 8, y, x_hi, x_lo, core)}
    y_dev = {1: device(z, (y + 1) % 4, x_hi, x_lo, core), -1: device(z, (y + 3) % 4, x_hi, x_lo, core)}

    barrier = pltpu.get_barrier_semaphore()
    for other in (sib_dev, z_dev[1], z_dev[-1], y_dev[1], y_dev[-1]):
        pl.semaphore_signal(barrier, inc=1, device_id=other, device_id_type=MESH)

    @pl.when(jnp.logical_not(stays))
    def _():
        pl.semaphore_signal(barrier, inc=1, device_id=swap_dev, device_id_type=MESH)

    stage[0:256, :] = k_ref[...]
    v32 = v_ref[...].astype(F32)
    stage[256:384, :] = v32[0:128, :].T.astype(BF16)
    stage[384:512, :] = v32[128:256, :].T.astype(BF16)

    role = (z * 4 + y) * 2 + core
    for n, chunk in enumerate(CHUNKS):
        for j, (dz, dy) in enumerate(chunk):
            for own in range(2):
                from_core = core if own == 0 else 1 - core
                origin = (((z + 8 - dz) % 8) * 4 + (y + 4 - dy) % 4) * 2 + from_core
                bias[n * 8 + own * 4 + j] = jnp.where(origin < role, 0.0, HIDE).astype(F32)

    @pl.when(stays)
    def _():
        pl.semaphore_wait(barrier, 5)

    @pl.when(jnp.logical_not(stays))
    def _():
        pl.semaphore_wait(barrier, 6)

    def spot_ref(dz, dy):
        n, j = PLACE[(dz, dy)]
        return kv.at[n, 0, j]

    def remote(src, dst, send, recv, target):
        return pltpu.make_async_remote_copy(
            src_ref=src, dst_ref=dst, send_sem=send, recv_sem=recv,
            device_id=target, device_id_type=MESH,
        )

    def swap(index, src, dst):
        return remote(src, dst, swap_s.at[index], swap_r.at[index], swap_dev)

    def local(index, src, dst):
        return pltpu.make_async_copy(src, dst, swap_r.at[index])

    def start_swap(index, src, dst):
        @pl.when(stays)
        def _():
            local(index, src, dst).start()

        @pl.when(jnp.logical_not(stays))
        def _():
            swap(index, src, dst).start()

    def wait_swap(index, src, dst):
        @pl.when(stays)
        def _():
            local(index, src, dst).wait()

        @pl.when(jnp.logical_not(stays))
        def _():
            swap(index, src, dst).wait()

    start_swap(0, stage, spot_ref(0, 0))
    start_swap(1, q_ref, q_raw)

    Z_INDEX = {1: 0, -1: 1, 2: 2, -2: 3, 3: 4, -3: 5}

    def z_copy(dz, half=None):
        step = 1 if (dz > 0 and half != 1) else -1
        if dz == 4:
            source = spot_ref(3 if half == 0 else -3, 0).at[pl.ds(half * 256, 256)]
            target = spot_ref(4, 0).at[pl.ds(half * 256, 256)]
            at = 6 + half
        else:
            source = spot_ref(dz - step, 0)
            target = spot_ref(dz, 0)
            at = Z_INDEX[dz]
        return remote(source, target, z_s.at[at], z_r.at[at], z_dev[step])

    def y_copy(dz, dy, half=None):
        base = DZ_ORDER.index(dz) * 4
        if dy == 2:
            step = 1 if half == 0 else -1
            source = spot_ref(dz, step).at[pl.ds(half * 256, 256)]
            target = spot_ref(dz, 2).at[pl.ds(half * 256, 256)]
            at = base + 2 + half
        else:
            step = dy
            source = spot_ref(dz, 0)
            target = spot_ref(dz, dy)
            at = base + (0 if dy == 1 else 1)
        return remote(source, target, y_s.at[at], y_r.at[at], y_dev[step])

    def sib_copy(n):
        return remote(kv.at[n, 0], kv.at[n, 1], sib_s.at[n], sib_r.at[n], sib_dev)

    def arrived(dz, dy):
        if (dz, dy) == (0, 0):
            pass
        elif dy == 0 and dz == 4:
            z_copy(4, 0).wait_recv()
            z_copy(4, 1).wait_recv()
        elif dy == 0:
            z_copy(dz).wait_recv()
        elif dy == 2:
            y_copy(dz, 2, 0).wait_recv()
            y_copy(dz, 2, 1).wait_recv()
        else:
            y_copy(dz, dy).wait_recv()
        if dy == 0:
            if dz == 0:
                z_copy(1).start()
                z_copy(-1).start()
            elif abs(dz) < 3:
                z_copy(dz + (1 if dz > 0 else -1)).start()
            elif dz == 3:
                z_copy(4, 0).start()
            elif dz == -3:
                z_copy(4, 1).start()
            y_copy(dz, 1).start()
            y_copy(dz, -1).start()
        elif dy == 1:
            y_copy(dz, 2, 0).start()
        elif dy == -1:
            y_copy(dz, 2, 1).start()

    def gather_chunk(n):
        for dz, dy in CHUNKS[n]:
            if (dz, dy) != (0, 0):
                arrived(dz, dy)
        sib_copy(n).start()

    wait_swap(0, stage, spot_ref(0, 0))
    arrived(0, 0)

    wait_swap(1, q_ref, q_raw)

    def flip(t, carry):
        at = pl.multiple_of(t * HD, HD)
        q_t[t] = q_raw[:, pl.ds(at, HD)].astype(F32).T.astype(BF16)
        return carry

    lax.fori_loop(0, TILES, flip, 0, unroll=True)

    ones = jnp.ones((16, 256), BF16)
    own_k = kv.at[0, 0, 0]

    def diagonal(t, carry):
        s = jnp.dot(own_k[0:256, :], q_t[t], preferred_element_type=F32)
        key = lax.broadcasted_iota(jnp.int32, (256, 256), 0)
        query = lax.broadcasted_iota(jnp.int32, (256, 256), 1)
        s = jnp.where(key <= query, s * SCALE, HIDE)
        best = jnp.max(s, axis=0, keepdims=True)
        p = jnp.exp2(s - best).astype(BF16)
        left = jnp.concatenate([own_k[256:384, :], own_k[384:512, :]], axis=1)
        left = jnp.concatenate([left, ones], axis=0)
        acc[t] = jnp.dot(left, p, preferred_element_type=F32)
        top[t] = jnp.broadcast_to(best, (8, 256))
        return carry

    lax.fori_loop(0, TILES, diagonal, 0, unroll=2)

    gather_chunk(0)
    sib_copy(0).wait_recv()

    def score(n, t, slot):
        k_all = kv[n, :, :, 0:256, :].reshape(2048, HD)
        s = jnp.dot(k_all, q_t[t], preferred_element_type=F32)
        scores[slot] = s
        best = None
        for block in range(8):
            part = jnp.max(s[block * 256:(block + 1) * 256].reshape(32, 8, 256), axis=0) + bias[n * 8 + block]
            best = part if best is None else jnp.maximum(best, part)
        tops[slot] = best

    def absorb(n, t, slot):
        old = top[t]
        new = jnp.maximum(old, jnp.max(tops[slot], axis=0, keepdims=True) * SCALE)
        top[t] = new
        fade = jnp.exp2(old - new)[:1]
        row = new[:1]
        pieces = []
        left = []
        for block in range(8):
            shift = row - bias[n * 8 + block]
            s = scores[slot, block * 256:(block + 1) * 256, :]
            pieces.append(jnp.exp2(s * SCALE - shift).astype(BF16))
            left.append(kv[n, block // 4, block % 4, 256:384, :])
            left.append(kv[n, block // 4, block % 4, 384:512, :])
        left = jnp.concatenate(left, axis=1)
        left = jnp.concatenate([left, jnp.ones((16, 2048), BF16)], axis=0)
        update = jnp.dot(left, jnp.concatenate(pieces, axis=0), preferred_element_type=F32)
        acc[t] = acc[t] * fade + update

    score(0, 0, 0)

    def pair(step, carry):
        n = step // 4
        part = step % 4
        t = part * 2
        for m in range(NCHUNK - 1):
            @pl.when((n == m) & (part == 2))
            def _():
                gather_chunk(m + 1)

        @pl.when((part == 3) & (n < NCHUNK - 1))
        def _():
            remote(kv.at[n + 1, 0], kv.at[n + 1, 1], sib_s.at[n + 1], sib_r.at[n + 1], sib_dev).wait_recv()

        score(n, t + 1, 1)
        absorb(n, t, 0)
        follow = jnp.minimum(step + 1, NCHUNK * 4 - 1)
        score(follow // 4, (follow % 4) * 2, 0)
        absorb(n, t + 1, 1)
        return carry

    lax.fori_loop(0, NCHUNK * 4, pair, 0)

    def finish(t, carry):
        at = pl.multiple_of(t * HD, HD)
        total = acc[t]
        mixed = total[0:128, :] / total[128:129, :]
        o_role[:, pl.ds(at, HD)] = mixed.T.astype(BF16)
        return carry

    lax.fori_loop(0, TILES, finish, 0, unroll=2)
    start_swap(2, o_role, o_ref)

    for dz in DZ_ORDER:
        if dz == 4:
            z_copy(4, 0).wait_send()
            z_copy(4, 1).wait_send()
        elif dz != 0:
            z_copy(dz).wait_send()
        y_copy(dz, 1).wait_send()
        y_copy(dz, -1).wait_send()
        y_copy(dz, 2, 0).wait_send()
        y_copy(dz, 2, 1).wait_send()
    for n in range(NCHUNK):
        sib_copy(n).wait_send()
    wait_swap(2, o_role, o_ref)


def attention(queries, keys, values):
    dma = pltpu.SemaphoreType.DMA
    return pl.pallas_call(
        attention_kernel,
        out_shape=jax.ShapeDtypeStruct(queries.shape, BF16),
        in_specs=[pl.BlockSpec(memory_space=pltpu.VMEM)] * 3,
        out_specs=pl.BlockSpec(memory_space=pltpu.VMEM),
        scratch_shapes=[
            pltpu.VMEM((512, HD), BF16),
            pltpu.VMEM((NCHUNK, 2, 4, 512, HD), BF16),
            pltpu.VMEM((ROWS, GROUP * HD), BF16),
            pltpu.VMEM((TILES, HD, 256), BF16),
            pltpu.VMEM((TILES, 144, 256), F32),
            pltpu.VMEM((TILES, 8, 256), F32),
            pltpu.VMEM((2, 2048, 256), F32),
            pltpu.VMEM((2, 8, 256), F32),
            pltpu.VMEM((ROWS, GROUP * HD), BF16),
            pltpu.SMEM((64,), F32),
            dma((3,)), dma((3,)), dma((8,)), dma((8,)), dma((32,)), dma((32,)), dma((NCHUNK,)), dma((NCHUNK,)),
        ],
        compiler_params=pltpu.CompilerParams(
            collective_id=0, has_side_effects=True, vmem_limit_bytes=48 * 2**20
        ),
        name="attention",
    )(queries, keys, values)


def score_kernel(
    att_ref, w_ref, w8_ref, pos_ref, col_ref, attr_ref, out_ref,
    block, other, fa, fb, part, part16, got, square, got_sq, r1, r2, r3,
    x_s, x_r, a_s, a_r, b_s, b_r, h_s, h_r, q_s, q_r, s1, t1, s2, t2, s3, t3,
):
    z, y, x_hi, x_lo, core = coords()
    ctx = lax.axis_index("ctx")
    head = lax.axis_index("head")
    me8 = x_hi * 4 + head
    x_dev = device(z, y, 1 - x_hi, x_lo, core)

    def z_at(step):
        return device((z + step) % 8, y, x_hi, x_lo, core)

    def y_at(step):
        return device(z, (y + step) % 4, x_hi, x_lo, core)

    def chip_at(step):
        other8 = (me8 + step) % 8
        return ((z * 4 + y) * 2 + other8 // 4, other8 % 4)

    barrier = pltpu.get_barrier_semaphore()
    for step in range(1, 8):
        pl.semaphore_signal(barrier, inc=1, device_id=z_at(step), device_id_type=MESH)
        pl.semaphore_signal(barrier, inc=1, device_id=chip_at(step), device_id_type=MESH)
    for step in range(1, 4):
        pl.semaphore_signal(barrier, inc=1, device_id=y_at(step), device_id_type=MESH)

    pos = pos_ref[...]
    col = col_ref[...]
    owner = pos // ROWS
    first = jnp.sum((col < owner * ROWS).astype(jnp.int32), axis=0, keepdims=True)
    step_id = lax.broadcasted_iota(jnp.int32, (1, 256), 1)
    rank = step_id - first
    slot_row = lax.broadcasted_iota(jnp.int32, (16, 256), 0)
    mine = (owner == ctx) & (rank + x_hi * CAP == slot_row)
    token = lax.broadcasted_iota(jnp.int32, (256, 256), 1)
    place = (col - ctx * ROWS == token)
    pick = jnp.dot(mine.astype(F32).astype(BF16), place.astype(F32).astype(BF16), preferred_element_type=F32)
    rows = jnp.dot(pick.astype(BF16), att_ref[...], preferred_element_type=F32)
    block[...] = rows.astype(BF16)

    pl.semaphore_wait(barrier, 17)

    def remote(src, dst, send, recv, target):
        return pltpu.make_async_remote_copy(
            src_ref=src, dst_ref=dst, send_sem=send, recv_sem=recv,
            device_id=target, device_id_type=MESH,
        )

    swap = remote(block, other, x_s, x_r, x_dev)
    swap.start()
    swap.wait()
    both = block[...] + other[...]
    fa[0, 0] = both[:, :512]
    fb[0, 0] = both[:, 512:]

    def copy_a(index, src, dst, target):
        return remote(src, dst, a_s.at[index], a_r.at[index], target)

    def copy_b(index, src, dst, target):
        return remote(src, dst, b_s.at[index], b_r.at[index], target)

    up, down = z_at(1), z_at(7)
    right, left = y_at(1), y_at(3)
    low, high = pl.ds(0, 2), pl.ds(2, 2)
    a_y1 = copy_a(0, fa.at[0, 0], fa.at[0, 1], right)
    a_y3 = copy_a(1, fa.at[0, 0], fa.at[0, 3], left)
    a_y2 = copy_a(2, fa.at[0, 1], fa.at[0, 2], right)
    a_z1 = copy_a(3, fa.at[0], fa.at[1], up)
    a_z7 = copy_a(4, fa.at[0], fa.at[7], down)
    a_z2 = copy_a(5, fa.at[1], fa.at[2], up)
    a_z6 = copy_a(6, fa.at[7], fa.at[6], down)
    a_z3 = copy_a(7, fa.at[2], fa.at[3], up)
    a_z5 = copy_a(8, fa.at[6], fa.at[5], down)
    a_4l = copy_a(9, fa.at[3, low], fa.at[4, low], up)
    a_4h = copy_a(10, fa.at[5, high], fa.at[4, high], down)
    b_z1 = copy_b(0, fb.at[0, 0], fb.at[1, 0], up)
    b_z7 = copy_b(1, fb.at[0, 0], fb.at[7, 0], down)
    b_z2 = copy_b(2, fb.at[1, 0], fb.at[2, 0], up)
    b_z6 = copy_b(3, fb.at[7, 0], fb.at[6, 0], down)
    b_z3 = copy_b(4, fb.at[2, 0], fb.at[3, 0], up)
    b_z5 = copy_b(5, fb.at[6, 0], fb.at[5, 0], down)
    b_z4 = copy_b(6, fb.at[3, 0], fb.at[4, 0], up)
    b_y1 = copy_b(7, fb.at[:, 0], fb.at[:, 1], right)
    b_y3 = copy_b(8, fb.at[:, 0], fb.at[:, 3], left)
    b_2l = copy_b(9, fb.at[pl.ds(0, 4), 1], fb.at[pl.ds(0, 4), 2], right)
    b_2h = copy_b(10, fb.at[pl.ds(4, 4), 3], fb.at[pl.ds(4, 4), 2], left)

    for c in (a_y1, a_y3, b_z1, b_z7):
        c.start()
    a_y1.wait_recv()
    a_y2.start()
    b_z1.wait_recv()
    b_z2.start()
    b_z7.wait_recv()
    b_z6.start()
    a_y3.wait_recv()
    a_y2.wait_recv()
    a_z1.start()
    a_z7.start()
    b_z2.wait_recv()
    b_z3.start()
    b_z6.wait_recv()
    b_z5.start()
    a_z1.wait_recv()
    a_z2.start()
    a_z7.wait_recv()
    a_z6.start()
    b_z3.wait_recv()
    b_z4.start()
    b_z5.wait_recv()
    b_z4.wait_recv()
    b_y1.start()
    b_y3.start()
    a_z2.wait_recv()
    a_z3.start()
    a_z6.wait_recv()
    a_z5.start()
    b_y1.wait_recv()
    b_2l.start()
    b_y3.wait_recv()
    b_2h.start()
    a_z3.wait_recv()
    a_4l.start()
    a_z5.wait_recv()
    a_4h.start()

    r = lax.broadcasted_iota(jnp.int32, (128, 256), 0)
    dz = head * 2 + r // 64
    zz = (z + 8 - dz) % 8
    yy = (y + 4 - (r // 16) % 4) % 4
    slot = ((zz * 4 + yy) * 2 + (r // 8) % 2) * CAP + r % CAP
    match = slot == owner * CAP + rank
    match32 = match.astype(F32)
    wanted = jnp.sum(jnp.where(match, (attr_ref[...] == ctx // 16).astype(F32), 0.0), axis=1, keepdims=True)

    b_2l.wait_recv()
    b_2h.wait_recv()
    a_4l.wait_recv()
    a_4h.wait_recv()

    half_a = fa[...].reshape(512, 512)
    half_b = fb[...].reshape(512, 512)
    partial = jnp.dot(half_a, w_ref[0:512, :], preferred_element_type=F32)
    partial = partial + jnp.dot(half_b, w_ref[512:1024, :], preferred_element_type=F32)
    part[...] = partial
    part16[...] = partial.astype(BF16)
    for j in range(4):
        both = jnp.zeros((128, 128), F32)
        for half in (fa, fb):
            rows32 = half[2 * j:2 * j + 2].reshape(128, 512).astype(F32)
            sq = rows32 * rows32
            for c in range(4):
                both = both + sq[:, c * 128:(c + 1) * 128]
        total = jnp.broadcast_to(jnp.sum(both, axis=1, keepdims=True), (128, 128))
        square[j] = total.T[0:8, :]

    def head_dev(step):
        return (ctx, (head + step) % 4)

    sends = []
    for step in range(1, 4):
        to = (head + step) % 4
        at = pl.ds(pl.multiple_of(to * 128, 128), 128)
        sends.append(remote(square.at[to], got_sq.at[step], q_s.at[step], q_r.at[step], head_dev(step)))
        sends.append(remote(part16.at[at], got.at[step], h_s.at[step], h_r.at[step], head_dev(step)))
    for c in sends:
        c.start()
    pre = part[pl.ds(pl.multiple_of(head * 128, 128), 128), :]
    squares = square[head]
    for c in sends:
        c.wait()
    for step in range(1, 4):
        pre = pre + got[step].astype(F32)
        squares = squares + got_sq[step]
    factor = lax.rsqrt(squares[0:1, :] / FEAT + NORM_EPS)
    factor = jnp.broadcast_to(factor, (128, 128)).T[:, 0:1]
    hidden = jnp.where(wanted > 0.5, jnp.maximum(pre * factor, 0.0), 0.0).astype(BF16)
    terms = lax.dot_general(w8_ref[...], hidden, (((1,), (1,)), ((), ())), preferred_element_type=F32)[0:8, :]
    mapped = jnp.dot(terms, match32, preferred_element_type=F32, precision=lax.Precision.HIGHEST)
    line = lax.broadcasted_iota(jnp.int32, (8, 128), 0)
    tile = jnp.where(line < 2, mapped[:, :128], mapped[:, 128:])

    def all_sum(value, buf, send, recv, me, count, at):
        buf[me] = value
        copies = []
        for step in range(1, count):
            copies.append(remote(buf.at[me], buf.at[me], send.at[step], recv.at[step], at(step)))
        for c in copies:
            c.start()
        for c in copies:
            c.wait_recv()
        total = buf[0]
        for i in range(1, count):
            total = total + buf[i]
        return total, copies

    tile, c1 = all_sum(tile, r1, s1, t1, me8, 8, chip_at)
    tile, c2 = all_sum(tile, r2, s2, t2, y, 4, y_at)
    tile, c3 = all_sum(tile, r3, s3, t3, z, 8, z_at)
    out_ref[...] = tile

    for c in c1 + c2 + c3:
        c.wait_send()
    for c in (a_y1, a_y3, a_y2, a_z1, a_z7, a_z2, a_z6, a_z3, a_z5, a_4l, a_4h):
        c.wait_send()
    for c in (b_z1, b_z7, b_z2, b_z6, b_z3, b_z5, b_z4, b_y1, b_y3, b_2l, b_2h):
        c.wait_send()


def step_scores(attended, w_in, w_out, step_pos, step_attr):
    dma = pltpu.SemaphoreType.DMA
    rows = jnp.concatenate([w_out.T, w_out.T], axis=0)
    w8 = jnp.concatenate([rows, jnp.zeros((12, 256), BF16)], axis=0)
    tile = pl.pallas_call(
        score_kernel,
        out_shape=jax.ShapeDtypeStruct((8, 128), F32),
        in_specs=[pl.BlockSpec(memory_space=pltpu.VMEM)] * 6,
        out_specs=pl.BlockSpec(memory_space=pltpu.VMEM),
        scratch_shapes=[
            pltpu.VMEM((16, 1024), BF16),
            pltpu.VMEM((16, 1024), BF16),
            pltpu.VMEM((8, 4, 16, 512), BF16),
            pltpu.VMEM((8, 4, 16, 512), BF16),
            pltpu.VMEM((512, 256), F32),
            pltpu.VMEM((512, 256), BF16),
            pltpu.VMEM((4, 128, 256), BF16),
            pltpu.VMEM((4, 8, 128), F32),
            pltpu.VMEM((4, 8, 128), F32),
            pltpu.VMEM((8, 8, 128), F32),
            pltpu.VMEM((4, 8, 128), F32),
            pltpu.VMEM((8, 8, 128), F32),
            dma, dma, dma((11,)), dma((11,)), dma((11,)), dma((11,)),
            dma((4,)), dma((4,)), dma((4,)), dma((4,)),
            dma((8,)), dma((8,)), dma((4,)), dma((4,)), dma((8,)), dma((8,)),
        ],
        compiler_params=pltpu.CompilerParams(
            collective_id=1, has_side_effects=True, vmem_limit_bytes=48 * 2**20
        ),
        name="step_scores",
    )(attended, w_in, w8, step_pos.reshape(1, 256), step_pos.reshape(256, 1), step_attr.reshape(1, 256))
    return jnp.concatenate([tile[0:2], tile[2:4]], axis=1).T


def body(queries, keys, values, w_in, w_out, step_pos, step_attr):
    attended = attention(queries, keys, values)
    return attended, step_scores(attended, w_in, w_out, step_pos, step_attr)


def solution(mesh):
    in_specs = (
        P("ctx", "head"),
        P("ctx", "head"),
        P("ctx", "head"),
        P("head", "ctx"),
        P("ctx", None),
        P(),
        P(),
    )
    out_specs = (P("ctx", "head"), P())
    return jax.shard_map(body, mesh=mesh, in_specs=in_specs, out_specs=out_specs, check_vma=False)
```

```python
import functools
import math

import jax
import jax.numpy as jnp
from jax import lax
from jax.experimental import pallas as pl
from jax.experimental.pallas import tpu as pltpu
from jax.sharding import PartitionSpec as P

HD = 128
GROUP = 8
ROWS = 256
HID = 4096
CAP = 8
FEAT = 4096
NORM_EPS = 1e-06
SCALE = HD ** -0.5 * math.log2(math.e)
HIDE = -1e30
MESH = pl.DeviceIdType.MESH
F32 = jnp.float32
BF16 = jnp.bfloat16

CHUNKS = (
    ((0, 0), (1, 0), (-1, 0), (0, 1)),
    ((0, -1), (2, 0), (-2, 0), (1, 1)),
    ((1, -1), (-1, 1), (-1, -1), (3, 0)),
    ((-3, 0), (2, 1), (2, -1), (-2, 1)),
    ((-2, -1), (4, 0), (3, 1), (3, -1)),
    ((-3, 1), (-3, -1), (4, 1), (4, -1)),
    ((0, 2), (1, 2), (-1, 2), (2, 2)),
    ((-2, 2), (3, 2), (-3, 2), (4, 2)),
)
PLACE = {spot: (n, j) for n, chunk in enumerate(CHUNKS) for j, spot in enumerate(chunk)}
DZ_ORDER = (0, 1, -1, 2, -2, 3, -3, 4)
TILES = GROUP
NCHUNK = len(CHUNKS)


def coords():
    ctx = lax.axis_index("ctx")
    head = lax.axis_index("head")
    return ctx // 8, (ctx // 2) % 4, ctx % 2, head // 2, head % 2


def device(z, y, x_hi, x_lo, core):
    return ((z * 4 + y) * 2 + x_hi, x_lo * 2 + core)


EVENT = (0, 2, 5, 8, 11, 14, 17, 20)
SPLIT = (21, 28, 32)


def fused_kernel(
    q_ref, k_ref, v_ref, w_ref, w_out_ref, pos_ref, attr_ref,
    o_ref, logit_ref,
    stage, v_in, kv, q_raw, q_t, acc, top, scores, tops, o_role, bias,
    qs_t, s_scores, s_acc, s_top, w_v,
    block, other, fa, fb, own_a, own_b, part, part16, got, square, got_sq, r1, r2, r3,
    load, swap_s, swap_r, z_s, z_r, y_s, y_r, sib_s, sib_r,
    x_s, x_r, a_s, a_r, b_s, b_r, h_s, h_r, g_s, g_r, s1, t1, s2, t2, s3, t3,
):
    z, y, x_hi, x_lo, core = coords()
    ctx = lax.axis_index("ctx")
    head = lax.axis_index("head")
    me8 = x_hi * 4 + head
    stays = x_hi == core
    sib_dev = device(z, y, x_hi, x_lo, 1 - core)

    def z_at(step):
        return device((z + step) % 8, y, x_hi, x_lo, core)

    def y_at(step):
        return device(z, (y + step) % 4, x_hi, x_lo, core)

    def chip_at(step):
        other8 = (me8 + step) % 8
        return ((z * 4 + y) * 2 + other8 // 4, other8 % 4)

    def flip_at(z_step, y_step):
        return device((z + z_step) % 8, (y + y_step) % 4, core, x_lo, x_hi)

    swap_dev = flip_at(0, 0)
    z_dev = {1: z_at(1), -1: z_at(7)}
    y_dev = {1: y_at(1), -1: y_at(3)}

    barrier = pltpu.get_barrier_semaphore()

    def greet(target):
        pl.semaphore_signal(barrier, inc=1, device_id=target, device_id_type=MESH)

    for step in range(1, 8):
        greet(z_at(step))
        greet(flip_at(step, 0))
        greet(chip_at(step))
    for step in range(1, 4):
        greet(y_at(step))
        greet(flip_at(0, step))

    get_k = pltpu.make_async_copy(k_ref, stage.at[pl.ds(0, 256)], load.at[0])
    get_v = pltpu.make_async_copy(v_ref, v_in, load.at[1])
    get_w = pltpu.make_async_copy(w_ref, w_v, load.at[2])
    get_v.start()
    get_k.start()
    get_w.start()

    role = (z * 4 + y) * 2 + core
    for n, chunk in enumerate(CHUNKS):
        for j, (dz, dy) in enumerate(chunk):
            for own in range(2):
                from_core = core if own == 0 else 1 - core
                origin = (((z + 8 - dz) % 8) * 4 + (y + 4 - dy) % 4) * 2 + from_core
                bias[n * 8 + own * 4 + j] = jnp.where(origin < role, 0.0, HIDE).astype(F32)

    get_v.wait()
    v32 = v_in[...].astype(F32)
    stage[256:384, :] = v32[0:128, :].T.astype(BF16)
    stage[384:512, :] = v32[128:256, :].T.astype(BF16)
    get_k.wait()

    pl.semaphore_wait(barrier, 27)

    def spot_ref(dz, dy):
        n, j = PLACE[(dz, dy)]
        return kv.at[n, 0, j]

    def remote(src, dst, send, recv, target):
        return pltpu.make_async_remote_copy(
            src_ref=src, dst_ref=dst, send_sem=send, recv_sem=recv,
            device_id=target, device_id_type=MESH,
        )

    def start_flip(src, dst, send, recv):
        @pl.when(stays)
        def _():
            pltpu.make_async_copy(src, dst, recv).start()

        @pl.when(jnp.logical_not(stays))
        def _():
            remote(src, dst, send, recv, swap_dev).start()

    def wait_flip(src, dst, send, recv):
        @pl.when(stays)
        def _():
            pltpu.make_async_copy(src, dst, recv).wait()

        @pl.when(jnp.logical_not(stays))
        def _():
            remote(src, dst, send, recv, swap_dev).wait()

    kv_flip = (stage, spot_ref(0, 0), swap_s.at[0], swap_r.at[0])
    q_flip = (q_ref, q_raw, swap_s.at[1], swap_r.at[1])
    o_flip = (o_role, o_ref, swap_s.at[2], swap_r.at[2])
    start_flip(*kv_flip)
    start_flip(*q_flip)

    Z_INDEX = {1: 0, -1: 1, 2: 2, -2: 3, 3: 4, -3: 5}

    def z_copy(dz, half=None):
        step = 1 if (dz > 0 and half != 1) else -1
        if dz == 4:
            source = spot_ref(3 if half == 0 else -3, 0).at[pl.ds(half * 256, 256)]
            target = spot_ref(4, 0).at[pl.ds(half * 256, 256)]
            at = 6 + half
        else:
            source = spot_ref(dz - step, 0)
            target = spot_ref(dz, 0)
            at = Z_INDEX[dz]
        return remote(source, target, z_s.at[at], z_r.at[at], z_dev[step])

    def y_copy(dz, dy, half=None):
        base = DZ_ORDER.index(dz) * 4
        if dy == 2:
            step = 1 if half == 0 else -1
            source = spot_ref(dz, step).at[pl.ds(half * 256, 256)]
            target = spot_ref(dz, 2).at[pl.ds(half * 256, 256)]
            at = base + 2 + half
        else:
            step = dy
            source = spot_ref(dz, 0)
            target = spot_ref(dz, dy)
            at = base + (0 if dy == 1 else 1)
        return remote(source, target, y_s.at[at], y_r.at[at], y_dev[step])

    def sib_copy(n):
        return remote(kv.at[n, 0], kv.at[n, 1], sib_s.at[n], sib_r.at[n], sib_dev)

    def arrived(dz, dy):
        if (dz, dy) == (0, 0):
            pass
        elif dy == 0 and dz == 4:
            z_copy(4, 0).wait_recv()
            z_copy(4, 1).wait_recv()
        elif dy == 0:
            z_copy(dz).wait_recv()
        elif dy == 2:
            y_copy(dz, 2, 0).wait_recv()
            y_copy(dz, 2, 1).wait_recv()
        else:
            y_copy(dz, dy).wait_recv()
        if dy == 0:
            if dz == 0:
                z_copy(1).start()
                z_copy(-1).start()
            elif abs(dz) < 3:
                z_copy(dz + (1 if dz > 0 else -1)).start()
            elif dz == 3:
                z_copy(4, 0).start()
            elif dz == -3:
                z_copy(4, 1).start()
            y_copy(dz, 1).start()
            y_copy(dz, -1).start()
        elif dy == 1:
            y_copy(dz, 2, 0).start()
        elif dy == -1:
            y_copy(dz, 2, 1).start()

    def gather_chunk(n):
        for dz, dy in CHUNKS[n]:
            if (dz, dy) != (0, 0):
                arrived(dz, dy)
        sib_copy(n).start()

    pos = pos_ref[...]
    col = jnp.broadcast_to(pos.astype(F32), (128, 256)).T[:, 0:1].astype(jnp.int32)
    owner = pos // ROWS
    first = jnp.sum((col < owner * ROWS).astype(jnp.int32), axis=0, keepdims=True)
    rank = lax.broadcasted_iota(jnp.int32, (1, 256), 1) - first
    owner_col = col // ROWS
    first_col = jnp.sum((pos < owner_col * ROWS).astype(jnp.int32), axis=1, keepdims=True)
    rank_col = lax.broadcasted_iota(jnp.int32, (256, 1), 0) - first_col
    lane = lax.broadcasted_iota(jnp.int32, (256, 128), 1)
    held = (owner_col == role) & (rank_col == lane % CAP)
    s_row = jnp.sum(jnp.where(held, col - role * ROWS, 0), axis=0, keepdims=True)
    mine = (owner == role) & (rank == lax.broadcasted_iota(jnp.int32, (16, 256), 0))
    place = col - role * ROWS == lax.broadcasted_iota(jnp.int32, (256, 256), 1)
    pick = jnp.dot(mine.astype(F32).astype(BF16), place.astype(F32).astype(BF16), preferred_element_type=F32)
    pick = pick.astype(BF16)

    wait_flip(*kv_flip)
    arrived(0, 0)
    wait_flip(*q_flip)

    def turn(t, carry):
        at = pl.multiple_of(t * HD, HD)
        q_t[t] = q_raw[:, pl.ds(at, HD)].astype(F32).T.astype(BF16)
        return carry

    lax.fori_loop(0, TILES, turn, 0, unroll=True)
    s_rows = jnp.dot(pick, q_raw[...], preferred_element_type=F32)
    stacked = [s_rows[0:8, h * HD:(h + 1) * HD] for h in range(GROUP)]
    stacked = jnp.concatenate(stacked + [jnp.zeros((64, HD), F32)], axis=0)
    qs_t[...] = stacked.T.astype(BF16)

    own_k = kv.at[0, 0, 0]

    def values_of(ref):
        return jnp.concatenate([ref[256:384, :], ref[384:512, :]], axis=1)

    def first_block(q, last):
        width = q.shape[1]
        s = jnp.dot(own_k[0:256, :], q, preferred_element_type=F32)
        key = lax.broadcasted_iota(jnp.int32, (256, width), 0)
        s = jnp.where(key <= last, s * SCALE, HIDE)
        best = jnp.max(s, axis=0, keepdims=True)
        p = jnp.exp2(s - best).astype(BF16)
        left = jnp.concatenate([values_of(own_k), jnp.ones((16, 256), BF16)], axis=0)
        return jnp.dot(left, p, preferred_element_type=F32), jnp.broadcast_to(best, (8, width))

    def diagonal(t, carry):
        query = lax.broadcasted_iota(jnp.int32, (256, 256), 1)
        acc[t], top[t] = first_block(q_t[t], query)
        return carry

    s_acc[...], s_top[...] = first_block(qs_t[...], s_row)
    lax.fori_loop(0, TILES, diagonal, 0, unroll=2)

    def keys_of(n):
        return kv[n, :, :, 0:256, :].reshape(2048, HD)

    def best_of(s, n):
        best = None
        for at in range(8):
            part_best = jnp.max(s[at * 256:(at + 1) * 256].reshape(32, 8, s.shape[1]), axis=0) + bias[n * 8 + at]
            best = part_best if best is None else jnp.maximum(best, part_best)
        return best

    def mix(n, s_of, row):
        pieces = []
        left = []
        for at in range(8):
            shift = row - bias[n * 8 + at]
            pieces.append(jnp.exp2(s_of(at) * SCALE - shift).astype(BF16))
            left.append(kv[n, at // 4, at % 4, 256:384, :])
            left.append(kv[n, at // 4, at % 4, 384:512, :])
        left = jnp.concatenate(left, axis=1)
        left = jnp.concatenate([left, jnp.ones((16, 2048), BF16)], axis=0)
        return jnp.dot(left, jnp.concatenate(pieces, axis=0), preferred_element_type=F32)

    def score(n, t, slot):
        s = jnp.dot(keys_of(n), q_t[t], preferred_element_type=F32)
        scores[slot] = s
        tops[slot] = best_of(s, n)

    def absorb(n, t, slot):
        old = top[t]
        new = jnp.maximum(old, jnp.max(tops[slot], axis=0, keepdims=True) * SCALE)
        top[t] = new
        fade = jnp.exp2(old - new)[:1]
        update = mix(n, lambda at: scores[slot, at * 256:(at + 1) * 256, :], new[:1])
        acc[t] = acc[t] * fade + update

    def step_rows(n):
        s = jnp.dot(keys_of(n), qs_t[...], preferred_element_type=F32)
        s_scores[...] = s
        old = s_top[...]
        new = jnp.maximum(old, jnp.max(best_of(s, n), axis=0, keepdims=True) * SCALE)
        s_top[...] = new
        fade = jnp.exp2(old - new)[:1]
        update = mix(n, lambda at: s_scores[at * 256:(at + 1) * 256, :], new[:1])
        s_acc[...] = s_acc[...] * fade + update

    def pair(step, carry):
        n = step // 4
        t = (step % 4) * 2
        score(n, t + 1, 1)
        absorb(n, t, 0)
        follow = jnp.minimum(step + 1, NCHUNK * 4 - 1)
        score(follow // 4, (follow % 4) * 2, 0)
        absorb(n, t + 1, 1)
        return carry

    def turn_a(step, carry):
        for m in range(1, NCHUNK):
            @pl.when(step == EVENT[m])
            def _():
                gather_chunk(m)

        due = jnp.int32(0)
        fresh = step == EVENT[1] + 1
        for m in range(1, NCHUNK):
            due = due + (step > EVENT[m]).astype(jnp.int32)
            fresh = fresh | (step == EVENT[m] + 1)

        @pl.when(fresh)
        def _():
            remote(kv.at[due, 0], kv.at[due, 1], sib_s.at[due], sib_r.at[due], sib_dev).wait_recv()
            step_rows(due)

        return pair(step, carry)

    gather_chunk(0)
    sib_copy(0).wait_recv()
    step_rows(0)
    score(0, 0, 0)
    lax.fori_loop(0, SPLIT[0], turn_a, 0)
    sib_copy(7).wait_recv()
    step_rows(7)

    done = s_acc[...]
    mixed = (done[0:128, :] / done[128:129, :]).T
    row8 = jnp.concatenate([mixed[h * 8:(h + 1) * 8, :] for h in range(GROUP)], axis=1)
    row16 = jnp.concatenate([row8, row8], axis=0)
    row_id = lax.broadcasted_iota(jnp.int32, (16, 1024), 0)
    block[...] = jnp.where(row_id // CAP == core, row16, 0.0).astype(BF16)
    pair_up = remote(block, other, x_s, x_r, sib_dev)
    pair_up.start()
    pair_up.wait()
    both = block[...] + other[...]
    own_a[...] = both[:, :512]
    own_b[...] = both[:, 512:]

    def copy_a(index, src, dst, target):
        return remote(src, dst, a_s.at[index], a_r.at[index], target)

    def copy_b(index, src, dst, target):
        return remote(src, dst, b_s.at[index], b_r.at[index], target)

    flip_b = (own_b, fb.at[0, 0], b_s.at[0], b_r.at[0])
    flip_a = (own_a, fa.at[0, 0], a_s.at[0], a_r.at[0])
    b_z = [copy_b(k, own_b, fb.at[k, 0], flip_at(k, 0)) for k in range(1, 8)]
    a_y = [copy_a(k, own_a, fa.at[0, k], flip_at(0, k)) for k in range(1, 4)]
    start_flip(*flip_a)
    start_flip(*flip_b)
    for c in a_y + b_z:
        c.start()

    lax.fori_loop(SPLIT[0], SPLIT[1], pair, 0)

    low, high = pl.ds(0, 2), pl.ds(2, 2)
    a_z = [copy_a(3 + k, fa.at[0], fa.at[d % 8], z_at(d % 8)) for k, d in ((1, 1), (2, -1), (3, 2), (4, -2))]
    a_far = [
        copy_a(8, fa.at[2], fa.at[3], z_at(1)),
        copy_a(9, fa.at[6], fa.at[5], z_at(7)),
        copy_a(10, fa.at[2, low], fa.at[4, low], z_at(2)),
        copy_a(11, fa.at[6, high], fa.at[4, high], z_at(6)),
    ]
    b_y = [copy_b(7 + k, fb.at[:, 0], fb.at[:, k], y_at(k)) for k in (1, 3, 2)]

    wait_flip(*flip_a)
    for c in a_y:
        c.wait_recv()
    for c in a_z:
        c.start()
    wait_flip(*flip_b)
    for c in b_z:
        c.wait_recv()
    for c in b_y:
        c.start()

    lax.fori_loop(SPLIT[1], SPLIT[2], pair, 0)

    def finish(t, carry):
        at = pl.multiple_of(t * HD, HD)
        total = acc[t]
        o_role[:, pl.ds(at, HD)] = (total[0:128, :] / total[128:129, :]).T.astype(BF16)
        return carry

    for c in a_z:
        c.wait_recv()
    for c in a_far:
        c.start()
    lax.fori_loop(0, TILES, finish, 0, unroll=2)
    start_flip(*o_flip)

    r = lax.broadcasted_iota(jnp.int32, (128, 256), 0)
    dz = head * 2 + r // 64
    zz = (z + 8 - dz) % 8
    yy = (y + 4 - (r // 16) % 4) % 4
    slot = ((zz * 4 + yy) * 2 + (r // 8) % 2) * CAP + r % CAP
    match = slot == owner * CAP + rank
    match32 = match.astype(F32)
    wanted = jnp.sum(jnp.where(match, (attr_ref[...] == ctx // 16).astype(F32), 0.0), axis=1, keepdims=True)

    w32 = w_out_ref[...].astype(F32)
    odd = lax.broadcasted_iota(jnp.int32, (256, 128), 1) % 2 == 1
    w16 = jnp.where(odd, w32[:, 1:2], w32[:, 0:1]).T[0:16, :].astype(BF16)
    get_w.wait()
    for c in b_y + a_far:
        c.wait_recv()

    half_a = fa[...].reshape(512, 512)
    half_b = fb[...].reshape(512, 512)
    partial = jnp.dot(half_a, w_v[0:512, :], preferred_element_type=F32)
    partial = partial + jnp.dot(half_b, w_v[512:1024, :], preferred_element_type=F32)
    part[...] = partial
    part16[...] = partial.astype(BF16)
    for j in range(4):
        summed = jnp.zeros((128, 128), F32)
        for half in (fa, fb):
            rows32 = half[2 * j:2 * j + 2].reshape(128, 512).astype(F32)
            sq = rows32 * rows32
            for c in range(4):
                summed = summed + sq[:, c * 128:(c + 1) * 128]
        total = jnp.broadcast_to(jnp.sum(summed, axis=1, keepdims=True), (128, 128))
        square[j] = total.T[0:8, :]

    def head_dev(step):
        return (ctx, (head + step) % 4)

    sends = []
    for step in range(1, 4):
        to = (head + step) % 4
        at = pl.ds(pl.multiple_of(to * 128, 128), 128)
        sends.append(remote(square.at[to], got_sq.at[step], g_s.at[step], g_r.at[step], head_dev(step)))
        sends.append(remote(part16.at[at], got.at[step], h_s.at[step], h_r.at[step], head_dev(step)))
    for c in sends:
        c.start()
    pre = part[pl.ds(pl.multiple_of(head * 128, 128), 128), :]
    squares = square[head]
    for c in sends:
        c.wait()
    for step in range(1, 4):
        pre = pre + got[step].astype(F32)
        squares = squares + got_sq[step]
    factor = lax.rsqrt(squares[0:1, :] / FEAT + NORM_EPS)
    factor = jnp.broadcast_to(factor, (128, 128)).T[:, 0:1]
    hidden = jnp.where(wanted > 0.5, jnp.maximum(pre * factor, 0.0), 0.0).astype(BF16)
    terms = lax.dot_general(w16, hidden, (((1,), (1,)), ((), ())), preferred_element_type=F32)[0:8, :]
    mapped = jnp.dot(terms, match32, preferred_element_type=F32, precision=lax.Precision.HIGHEST)
    line = lax.broadcasted_iota(jnp.int32, (8, 128), 0)
    tile = jnp.where(line < 2, mapped[:, :128], mapped[:, 128:])

    def all_sum(value, buf, send, recv, me, count, at):
        buf[me] = value
        copies = []
        for step in range(1, count):
            copies.append(remote(buf.at[me], buf.at[me], send.at[step], recv.at[step], at(step)))
        for c in copies:
            c.start()
        for c in copies:
            c.wait_recv()
        total = buf[0]
        for i in range(1, count):
            total = total + buf[i]
        return total, copies

    tile, c1 = all_sum(tile, r1, s1, t1, me8, 8, chip_at)
    tile, c2 = all_sum(tile, r2, s2, t2, y, 4, y_at)
    tile, c3 = all_sum(tile, r3, s3, t3, z, 8, z_at)
    logit_ref[...] = tile

    for c in c1 + c2 + c3 + a_y + a_z + a_far + b_z + b_y:
        c.wait_send()
    for dz in DZ_ORDER:
        if dz == 4:
            z_copy(4, 0).wait_send()
            z_copy(4, 1).wait_send()
        elif dz != 0:
            z_copy(dz).wait_send()
        y_copy(dz, 1).wait_send()
        y_copy(dz, -1).wait_send()
        y_copy(dz, 2, 0).wait_send()
        y_copy(dz, 2, 1).wait_send()
    for n in range(NCHUNK):
        sib_copy(n).wait_send()
    wait_flip(*o_flip)


def body(queries, keys, values, w_in, w_out, step_pos, step_attr):
    dma = pltpu.SemaphoreType.DMA
    vmem = pltpu.VMEM
    here = pl.BlockSpec(memory_space=pltpu.VMEM)
    away = pl.BlockSpec(memory_space=pl.ANY)
    attended, tile = pl.pallas_call(
        fused_kernel,
        out_shape=(
            jax.ShapeDtypeStruct(queries.shape, BF16),
            jax.ShapeDtypeStruct((8, 128), F32),
        ),
        in_specs=[away] * 4 + [here] * 3,
        out_specs=(here, here),
        scratch_shapes=[
            vmem((512, HD), BF16),
            vmem((ROWS, HD), BF16),
            vmem((NCHUNK, 2, 4, 512, HD), BF16),
            vmem((ROWS, GROUP * HD), BF16),
            vmem((TILES, HD, 256), BF16),
            vmem((TILES, 144, 256), F32),
            vmem((TILES, 8, 256), F32),
            vmem((2, 2048, 256), F32),
            vmem((2, 8, 256), F32),
            vmem((ROWS, GROUP * HD), BF16),
            pltpu.SMEM((64,), F32),
            vmem((HD, 128), BF16),
            vmem((2048, 128), F32),
            vmem((144, 128), F32),
            vmem((8, 128), F32),
            vmem((1024, 256), BF16),
            vmem((16, 1024), BF16),
            vmem((16, 1024), BF16),
            vmem((8, 4, 16, 512), BF16),
            vmem((8, 4, 16, 512), BF16),
            vmem((16, 512), BF16),
            vmem((16, 512), BF16),
            vmem((512, 256), F32),
            vmem((512, 256), BF16),
            vmem((4, 128, 256), BF16),
            vmem((4, 8, 128), F32),
            vmem((4, 8, 128), F32),
            vmem((8, 8, 128), F32),
            vmem((4, 8, 128), F32),
            vmem((8, 8, 128), F32),
            dma((3,)), dma((3,)), dma((3,)), dma((8,)), dma((8,)), dma((32,)), dma((32,)),
            dma((NCHUNK,)), dma((NCHUNK,)),
            dma, dma, dma((12,)), dma((12,)), dma((11,)), dma((11,)),
            dma((4,)), dma((4,)), dma((4,)), dma((4,)),
            dma((8,)), dma((8,)), dma((4,)), dma((4,)), dma((8,)), dma((8,)),
        ],
        compiler_params=pltpu.CompilerParams(
            collective_id=0, has_side_effects=True, vmem_limit_bytes=60 * 2**20
        ),
        name="trace_scores",
    )(queries, keys, values, w_in, w_out, step_pos.reshape(1, 256), step_attr.reshape(1, 256))
    return attended, jnp.concatenate([tile[0:2], tile[2:4]], axis=1).T


def solution(mesh):
    in_specs = (
        P("ctx", "head"),
        P("ctx", "head"),
        P("ctx", "head"),
        P("head", "ctx"),
        P("ctx", None),
        P(),
        P(),
    )
    out_specs = (P("ctx", "head"), P())
    return jax.shard_map(body, mesh=mesh, in_specs=in_specs, out_specs=out_specs, check_vma=False)
```

```python
import functools
import math

import jax
import jax.numpy as jnp
from jax import lax
from jax.experimental import pallas as pl
from jax.experimental.pallas import tpu as pltpu
from jax.sharding import PartitionSpec as P

HD = 128
GROUP = 8
ROWS = 256
HID = 4096
CAP = 8
FEAT = 4096
NORM_EPS = 1e-06
SCALE = HD ** -0.5 * math.log2(math.e)
HIDE = -1e30
MESH = pl.DeviceIdType.MESH
F32 = jnp.float32
BF16 = jnp.bfloat16

CHUNKS = (
    ((0, 0), (1, 0), (-1, 0), (0, 1)),
    ((0, -1), (2, 0), (-2, 0), (1, 1)),
    ((1, -1), (-1, 1), (-1, -1), (3, 0)),
    ((-3, 0), (2, 1), (2, -1), (-2, 1)),
    ((-2, -1), (4, 0), (3, 1), (3, -1)),
    ((-3, 1), (-3, -1), (4, 1), (4, -1)),
    ((0, 2), (1, 2), (-1, 2), (2, 2)),
    ((-2, 2), (3, 2), (-3, 2), (4, 2)),
)
PLACE = {spot: (n, j) for n, chunk in enumerate(CHUNKS) for j, spot in enumerate(chunk)}
DZ_ORDER = (0, 1, -1, 2, -2, 3, -3, 4)
TILES = GROUP
NCHUNK = len(CHUNKS)


def coords():
    ctx = lax.axis_index("ctx")
    head = lax.axis_index("head")
    return ctx // 8, (ctx // 2) % 4, ctx % 2, head // 2, head % 2


def device(z, y, x_hi, x_lo, core):
    return ((z * 4 + y) * 2 + x_hi, x_lo * 2 + core)


EVENT = (0, 0, 0, 3, 5, 8, 10, 13)
SPLIT = (14, 18, 21, 24, 29, 32)


def fused_kernel(
    q_ref, k_ref, v_ref, w_ref, w_out_ref, pos_ref, attr_ref,
    o_ref, logit_ref,
    stage, v_in, kv, q_raw, q_t, acc, top, scores, tops, o_role, bias,
    qs_t, s_scores, s_acc, s_top, w_v,
    block, other, fa, fb, own_a, own_b, part, part16, got, square, got_sq, r1, r2, r3,
    load, swap_s, swap_r, z_s, z_r, y_s, y_r, sib_s, sib_r,
    x_s, x_r, a_s, a_r, b_s, b_r, h_s, h_r, g_s, g_r, s1, t1, s2, t2, s3, t3,
):
    z, y, x_hi, x_lo, core = coords()
    ctx = lax.axis_index("ctx")
    head = lax.axis_index("head")
    me8 = x_hi * 4 + head
    stays = x_hi == core
    sib_dev = device(z, y, x_hi, x_lo, 1 - core)

    def z_at(step):
        return device((z + step) % 8, y, x_hi, x_lo, core)

    def y_at(step):
        return device(z, (y + step) % 4, x_hi, x_lo, core)

    def chip_at(step):
        other8 = (me8 + step) % 8
        return ((z * 4 + y) * 2 + other8 // 4, other8 % 4)

    def flip_at(z_step, y_step):
        return device((z + z_step) % 8, (y + y_step) % 4, core, x_lo, x_hi)

    swap_dev = flip_at(0, 0)
    z_dev = {1: z_at(1), -1: z_at(7)}
    y_dev = {1: y_at(1), -1: y_at(3)}

    barrier = pltpu.get_barrier_semaphore()

    def greet(target):
        pl.semaphore_signal(barrier, inc=1, device_id=target, device_id_type=MESH)

    for step in range(1, 8):
        greet(z_at(step))
        greet(flip_at(step, 0))
        greet(chip_at(step))
    for step in range(1, 4):
        greet(y_at(step))
        greet(flip_at(0, step))

    get_k = pltpu.make_async_copy(k_ref, stage.at[pl.ds(0, 256)], load.at[0])
    get_v = pltpu.make_async_copy(v_ref, v_in, load.at[1])
    get_w = pltpu.make_async_copy(w_ref, w_v, load.at[2])
    get_v.start()
    get_k.start()
    get_w.start()

    role = (z * 4 + y) * 2 + core
    for n, chunk in enumerate(CHUNKS):
        for j, (dz, dy) in enumerate(chunk):
            for own in range(2):
                from_core = core if own == 0 else 1 - core
                origin = (((z + 8 - dz) % 8) * 4 + (y + 4 - dy) % 4) * 2 + from_core
                bias[n * 8 + own * 4 + j] = jnp.where(origin < role, 0.0, HIDE).astype(F32)

    get_v.wait()
    v32 = v_in[...].astype(F32)
    stage[256:384, :] = v32[0:128, :].T.astype(BF16)
    stage[384:512, :] = v32[128:256, :].T.astype(BF16)
    get_k.wait()

    pl.semaphore_wait(barrier, 27)

    def spot_ref(dz, dy):
        n, j = PLACE[(dz, dy)]
        return kv.at[n, 0, j]

    def remote(src, dst, send, recv, target):
        return pltpu.make_async_remote_copy(
            src_ref=src, dst_ref=dst, send_sem=send, recv_sem=recv,
            device_id=target, device_id_type=MESH,
        )

    def start_flip(src, dst, send, recv):
        @pl.when(stays)
        def _():
            pltpu.make_async_copy(src, dst, recv).start()

        @pl.when(jnp.logical_not(stays))
        def _():
            remote(src, dst, send, recv, swap_dev).start()

    def wait_flip(src, dst, send, recv):
        @pl.when(stays)
        def _():
            pltpu.make_async_copy(src, dst, recv).wait()

        @pl.when(jnp.logical_not(stays))
        def _():
            remote(src, dst, send, recv, swap_dev).wait()

    kv_flip = (stage, spot_ref(0, 0), swap_s.at[0], swap_r.at[0])
    q_flip = (q_ref, q_raw, swap_s.at[1], swap_r.at[1])
    o_flip = (o_role, o_ref, swap_s.at[2], swap_r.at[2])
    start_flip(*kv_flip)

    Z_INDEX = {1: 0, -1: 1, 2: 2, -2: 3, 3: 4, -3: 5}

    def z_copy(dz, half=None):
        step = 1 if (dz > 0 and half != 1) else -1
        if dz == 4:
            source = spot_ref(3 if half == 0 else -3, 0).at[pl.ds(half * 256, 256)]
            target = spot_ref(4, 0).at[pl.ds(half * 256, 256)]
            at = 6 + half
        else:
            source = spot_ref(dz - step, 0)
            target = spot_ref(dz, 0)
            at = Z_INDEX[dz]
        return remote(source, target, z_s.at[at], z_r.at[at], z_dev[step])

    def y_copy(dz, dy, half=None):
        base = DZ_ORDER.index(dz) * 4
        if dy == 2:
            step = 1 if half == 0 else -1
            source = spot_ref(dz, step).at[pl.ds(half * 256, 256)]
            target = spot_ref(dz, 2).at[pl.ds(half * 256, 256)]
            at = base + 2 + half
        else:
            step = dy
            source = spot_ref(dz, 0)
            target = spot_ref(dz, dy)
            at = base + (0 if dy == 1 else 1)
        return remote(source, target, y_s.at[at], y_r.at[at], y_dev[step])

    def sib_copy(n):
        return remote(kv.at[n, 0], kv.at[n, 1], sib_s.at[n], sib_r.at[n], sib_dev)

    def arrived(dz, dy):
        if (dz, dy) == (0, 0):
            pass
        elif dy == 0 and dz == 4:
            z_copy(4, 0).wait_recv()
            z_copy(4, 1).wait_recv()
        elif dy == 0:
            z_copy(dz).wait_recv()
        elif dy == 2:
            y_copy(dz, 2, 0).wait_recv()
            y_copy(dz, 2, 1).wait_recv()
        else:
            y_copy(dz, dy).wait_recv()
        if dy == 0:
            if dz == 0:
                z_copy(1).start()
                z_copy(-1).start()
            elif abs(dz) < 3:
                z_copy(dz + (1 if dz > 0 else -1)).start()
            elif dz == 3:
                z_copy(4, 0).start()
            elif dz == -3:
                z_copy(4, 1).start()
            y_copy(dz, 1).start()
            y_copy(dz, -1).start()
        elif dy == 1:
            y_copy(dz, 2, 0).start()
        elif dy == -1:
            y_copy(dz, 2, 1).start()

    def gather_chunk(n):
        for dz, dy in CHUNKS[n]:
            if (dz, dy) != (0, 0):
                arrived(dz, dy)
        sib_copy(n).start()

    wait_flip(*kv_flip)
    arrived(0, 0)
    start_flip(*q_flip)

    pos = pos_ref[...]
    col = jnp.broadcast_to(pos.astype(F32), (128, 256)).T[:, 0:1].astype(jnp.int32)
    owner = pos // ROWS
    first = jnp.sum((col < owner * ROWS).astype(jnp.int32), axis=0, keepdims=True)
    rank = lax.broadcasted_iota(jnp.int32, (1, 256), 1) - first
    owner_col = col // ROWS
    first_col = jnp.sum((pos < owner_col * ROWS).astype(jnp.int32), axis=1, keepdims=True)
    rank_col = lax.broadcasted_iota(jnp.int32, (256, 1), 0) - first_col
    lane = lax.broadcasted_iota(jnp.int32, (256, 128), 1)
    held = (owner_col == role) & (rank_col == lane % CAP)
    s_row = jnp.sum(jnp.where(held, col - role * ROWS, 0), axis=0, keepdims=True)
    mine = (owner == role) & (rank == lax.broadcasted_iota(jnp.int32, (16, 256), 0))
    place = col - role * ROWS == lax.broadcasted_iota(jnp.int32, (256, 256), 1)
    pick = jnp.dot(mine.astype(F32).astype(BF16), place.astype(F32).astype(BF16), preferred_element_type=F32)
    pick = pick.astype(BF16)

    gather_chunk(0)
    wait_flip(*q_flip)

    def turn(t, carry):
        at = pl.multiple_of(t * HD, HD)
        q_t[t] = q_raw[:, pl.ds(at, HD)].astype(F32).T.astype(BF16)
        return carry

    lax.fori_loop(0, TILES, turn, 0, unroll=True)
    s_rows = jnp.dot(pick, q_raw[...], preferred_element_type=F32)
    stacked = [s_rows[0:8, h * HD:(h + 1) * HD] for h in range(GROUP)]
    stacked = jnp.concatenate(stacked + [jnp.zeros((64, HD), F32)], axis=0)
    qs_t[...] = stacked.T.astype(BF16)

    own_k = kv.at[0, 0, 0]

    def values_of(ref):
        return jnp.concatenate([ref[256:384, :], ref[384:512, :]], axis=1)

    def first_block(q, last):
        width = q.shape[1]
        s = jnp.dot(own_k[0:256, :], q, preferred_element_type=F32)
        key = lax.broadcasted_iota(jnp.int32, (256, width), 0)
        s = jnp.where(key <= last, s * SCALE, HIDE)
        best = jnp.max(s, axis=0, keepdims=True)
        p = jnp.exp2(s - best).astype(BF16)
        left = jnp.concatenate([values_of(own_k), jnp.ones((16, 256), BF16)], axis=0)
        return jnp.dot(left, p, preferred_element_type=F32), jnp.broadcast_to(best, (8, width))

    def diagonal(t, carry):
        query = lax.broadcasted_iota(jnp.int32, (256, 256), 1)
        acc[t], top[t] = first_block(q_t[t], query)
        return carry

    s_acc[...], s_top[...] = first_block(qs_t[...], s_row)
    gather_chunk(1)
    lax.fori_loop(0, TILES, diagonal, 0, unroll=2)

    def keys_of(n):
        return kv[n, :, :, 0:256, :].reshape(2048, HD)

    def best_of(s, n):
        best = None
        for at in range(8):
            part_best = jnp.max(s[at * 256:(at + 1) * 256].reshape(32, 8, s.shape[1]), axis=0) + bias[n * 8 + at]
            best = part_best if best is None else jnp.maximum(best, part_best)
        return best

    def mix(n, s_of, row):
        pieces = []
        left = []
        for at in range(8):
            shift = row - bias[n * 8 + at]
            pieces.append(jnp.exp2(s_of(at) * SCALE - shift).astype(BF16))
            left.append(kv[n, at // 4, at % 4, 256:384, :])
            left.append(kv[n, at // 4, at % 4, 384:512, :])
        left = jnp.concatenate(left, axis=1)
        left = jnp.concatenate([left, jnp.ones((16, 2048), BF16)], axis=0)
        return jnp.dot(left, jnp.concatenate(pieces, axis=0), preferred_element_type=F32)

    def score(n, t, slot):
        s = jnp.dot(keys_of(n), q_t[t], preferred_element_type=F32)
        scores[slot] = s
        tops[slot] = best_of(s, n)

    def absorb(n, t, slot):
        old = top[t]
        new = jnp.maximum(old, jnp.max(tops[slot], axis=0, keepdims=True) * SCALE)
        top[t] = new
        fade = jnp.exp2(old - new)[:1]
        update = mix(n, lambda at: scores[slot, at * 256:(at + 1) * 256, :], new[:1])
        acc[t] = acc[t] * fade + update

    def step_rows(n):
        s = jnp.dot(keys_of(n), qs_t[...], preferred_element_type=F32)
        s_scores[...] = s
        old = s_top[...]
        new = jnp.maximum(old, jnp.max(best_of(s, n), axis=0, keepdims=True) * SCALE)
        s_top[...] = new
        fade = jnp.exp2(old - new)[:1]
        update = mix(n, lambda at: s_scores[at * 256:(at + 1) * 256, :], new[:1])
        s_acc[...] = s_acc[...] * fade + update

    def pair(step, carry):
        n = step // 4
        t = (step % 4) * 2
        score(n, t + 1, 1)
        absorb(n, t, 0)
        follow = jnp.minimum(step + 1, NCHUNK * 4 - 1)
        score(follow // 4, (follow % 4) * 2, 0)
        absorb(n, t + 1, 1)
        return carry

    def turn_a(step, carry):
        for m in range(2, NCHUNK):
            @pl.when(step == EVENT[m])
            def _():
                gather_chunk(m)

        due = jnp.int32(1)
        fresh = step == EVENT[2] + 1
        for m in range(2, NCHUNK):
            due = due + (step > EVENT[m]).astype(jnp.int32)
            fresh = fresh | (step == EVENT[m] + 1)

        @pl.when(fresh)
        def _():
            remote(kv.at[due, 0], kv.at[due, 1], sib_s.at[due], sib_r.at[due], sib_dev).wait_recv()
            step_rows(due)

        return pair(step, carry)

    sib_copy(0).wait_recv()
    step_rows(0)
    sib_copy(1).wait_recv()
    step_rows(1)
    score(0, 0, 0)
    lax.fori_loop(0, SPLIT[0], turn_a, 0)
    sib_copy(7).wait_recv()
    step_rows(7)

    done = s_acc[...]
    mixed = (done[0:128, :] / done[128:129, :]).T
    row8 = jnp.concatenate([mixed[h * 8:(h + 1) * 8, :] for h in range(GROUP)], axis=1)
    row16 = jnp.concatenate([row8, row8], axis=0)
    row_id = lax.broadcasted_iota(jnp.int32, (16, 1024), 0)
    block[...] = jnp.where(row_id // CAP == core, row16, 0.0).astype(BF16)
    pair_up = remote(block, other, x_s, x_r, sib_dev)
    pair_up.start()
    pair_up.wait()
    both = block[...] + other[...]
    own_a[...] = both[:, :512]
    own_b[...] = both[:, 512:]

    def copy_a(index, src, dst, target):
        return remote(src, dst, a_s.at[index], a_r.at[index], target)

    def copy_b(index, src, dst, target):
        return remote(src, dst, b_s.at[index], b_r.at[index], target)

    flip_b = (own_b, fb.at[0, 0], b_s.at[0], b_r.at[0])
    flip_a = (own_a, fa.at[0, 0], a_s.at[0], a_r.at[0])
    b_z = [copy_b(k, own_b, fb.at[k, 0], flip_at(k, 0)) for k in range(1, 8)]
    a_y = [copy_a(k, own_a, fa.at[0, k], flip_at(0, k)) for k in range(1, 4)]
    start_flip(*flip_a)
    start_flip(*flip_b)
    for c in a_y + b_z:
        c.start()

    low, high = pl.ds(0, 2), pl.ds(2, 2)
    a_z = [copy_a(3 + k, fa.at[0], fa.at[d % 8], z_at(d % 8)) for k, d in ((1, 1), (2, -1), (3, 2), (4, -2))]
    a_far = [
        copy_a(8, fa.at[2], fa.at[3], z_at(1)),
        copy_a(9, fa.at[6], fa.at[5], z_at(7)),
        copy_a(10, fa.at[2, low], fa.at[4, low], z_at(2)),
        copy_a(11, fa.at[6, high], fa.at[4, high], z_at(6)),
    ]
    b_y = [copy_b(7 + k, fb.at[:, 0], fb.at[:, k], y_at(k)) for k in (1, 3, 2)]

    lax.fori_loop(SPLIT[0], SPLIT[1], pair, 0)
    wait_flip(*flip_a)
    for c in a_y:
        c.wait_recv()
    for c in a_z:
        c.start()
    lax.fori_loop(SPLIT[1], SPLIT[2], pair, 0)
    wait_flip(*flip_b)
    for c in b_z:
        c.wait_recv()
    for c in b_y:
        c.start()
    lax.fori_loop(SPLIT[2], SPLIT[3], pair, 0)

    def finish(t, carry):
        at = pl.multiple_of(t * HD, HD)
        total = acc[t]
        o_role[:, pl.ds(at, HD)] = (total[0:128, :] / total[128:129, :]).T.astype(BF16)
        return carry

    for c in a_z:
        c.wait_recv()
    for c in a_far:
        c.start()
    lax.fori_loop(SPLIT[3], SPLIT[4], pair, 0)

    r = lax.broadcasted_iota(jnp.int32, (128, 256), 0)
    dz = head * 2 + r // 64
    zz = (z + 8 - dz) % 8
    yy = (y + 4 - (r // 16) % 4) % 4
    slot = ((zz * 4 + yy) * 2 + (r // 8) % 2) * CAP + r % CAP
    match = slot == owner * CAP + rank
    match32 = match.astype(F32)
    wanted = jnp.sum(jnp.where(match, (attr_ref[...] == ctx // 16).astype(F32), 0.0), axis=1, keepdims=True)

    w32 = w_out_ref[...].astype(F32)
    odd = lax.broadcasted_iota(jnp.int32, (16, 256), 0) % 2 == 1
    w16 = jnp.where(odd, w32[1:2, :], w32[0:1, :]).astype(BF16)
    get_w.wait()
    for c in b_y + a_far:
        c.wait_recv()

    half_a = fa[...].reshape(512, 512)
    half_b = fb[...].reshape(512, 512)
    partial = jnp.dot(half_a, w_v[0:512, :], preferred_element_type=F32)
    partial = partial + jnp.dot(half_b, w_v[512:1024, :], preferred_element_type=F32)
    part[...] = partial
    part16[...] = partial.astype(BF16)
    for j in range(4):
        summed = jnp.zeros((128, 128), F32)
        for half in (fa, fb):
            rows32 = half[2 * j:2 * j + 2].reshape(128, 512).astype(F32)
            sq = rows32 * rows32
            for c in range(4):
                summed = summed + sq[:, c * 128:(c + 1) * 128]
        total = jnp.broadcast_to(jnp.sum(summed, axis=1, keepdims=True), (128, 128))
        square[j] = total.T[0:8, :]

    def head_dev(step):
        return (ctx, (head + step) % 4)

    sends = []
    for step in range(1, 4):
        to = (head + step) % 4
        at = pl.ds(pl.multiple_of(to * 128, 128), 128)
        sends.append(remote(square.at[to], got_sq.at[step], g_s.at[step], g_r.at[step], head_dev(step)))
        sends.append(remote(part16.at[at], got.at[step], h_s.at[step], h_r.at[step], head_dev(step)))
    for c in sends:
        c.start()
    lax.fori_loop(SPLIT[4], SPLIT[5], pair, 0)
    pre = part[pl.ds(pl.multiple_of(head * 128, 128), 128), :]
    squares = square[head]
    for c in sends:
        c.wait()
    for step in range(1, 4):
        pre = pre + got[step].astype(F32)
        squares = squares + got_sq[step]
    factor = lax.rsqrt(squares[0:1, :] / FEAT + NORM_EPS)
    factor = jnp.broadcast_to(factor, (128, 128)).T[:, 0:1]
    hidden = jnp.where(wanted > 0.5, jnp.maximum(pre * factor, 0.0), 0.0).astype(BF16)
    terms = lax.dot_general(w16, hidden, (((1,), (1,)), ((), ())), preferred_element_type=F32)[0:8, :]
    mapped = jnp.dot(terms, match32, preferred_element_type=F32, precision=lax.Precision.HIGHEST)
    line = lax.broadcasted_iota(jnp.int32, (8, 128), 0)
    tile = jnp.where(line < 2, mapped[:, :128], mapped[:, 128:])

    def all_sum(value, buf, send, recv, me, count, at, beside=None):
        buf[me] = value
        copies = []
        for step in range(1, count):
            copies.append(remote(buf.at[me], buf.at[me], send.at[step], recv.at[step], at(step)))
        for c in copies:
            c.start()
        if beside is not None:
            beside()
        for c in copies:
            c.wait_recv()
        total = buf[0]
        for i in range(1, count):
            total = total + buf[i]
        return total, copies

    def hand_back():
        lax.fori_loop(0, TILES, finish, 0, unroll=2)
        start_flip(*o_flip)

    tile, c1 = all_sum(tile, r1, s1, t1, me8, 8, chip_at, hand_back)
    tile, c2 = all_sum(tile, r2, s2, t2, y, 4, y_at)
    tile, c3 = all_sum(tile, r3, s3, t3, z, 8, z_at)
    logit_ref[:, 0:128] = tile[0:2, :]
    logit_ref[:, 128:256] = tile[2:4, :]

    for c in c1 + c2 + c3 + a_y + a_z + a_far + b_z + b_y:
        c.wait_send()
    for dz in DZ_ORDER:
        if dz == 4:
            z_copy(4, 0).wait_send()
            z_copy(4, 1).wait_send()
        elif dz != 0:
            z_copy(dz).wait_send()
        y_copy(dz, 1).wait_send()
        y_copy(dz, -1).wait_send()
        y_copy(dz, 2, 0).wait_send()
        y_copy(dz, 2, 1).wait_send()
    for n in range(NCHUNK):
        sib_copy(n).wait_send()
    wait_flip(*o_flip)


def body(queries, keys, values, w_in, w_out, step_pos, step_attr):
    dma = pltpu.SemaphoreType.DMA
    vmem = pltpu.VMEM
    here = pl.BlockSpec(memory_space=pltpu.VMEM)
    away = pl.BlockSpec(memory_space=pl.ANY)
    attended, logits = pl.pallas_call(
        fused_kernel,
        out_shape=(
            jax.ShapeDtypeStruct(queries.shape, BF16),
            jax.ShapeDtypeStruct((2, 256), F32),
        ),
        in_specs=[away] * 4 + [here] * 3,
        out_specs=(here, here),
        scratch_shapes=[
            vmem((512, HD), BF16),
            vmem((ROWS, HD), BF16),
            vmem((NCHUNK, 2, 4, 512, HD), BF16),
            vmem((ROWS, GROUP * HD), BF16),
            vmem((TILES, HD, 256), BF16),
            vmem((TILES, 144, 256), F32),
            vmem((TILES, 8, 256), F32),
            vmem((2, 2048, 256), F32),
            vmem((2, 8, 256), F32),
            vmem((ROWS, GROUP * HD), BF16),
            pltpu.SMEM((64,), F32),
            vmem((HD, 128), BF16),
            vmem((2048, 128), F32),
            vmem((144, 128), F32),
            vmem((8, 128), F32),
            vmem((1024, 256), BF16),
            vmem((16, 1024), BF16),
            vmem((16, 1024), BF16),
            vmem((8, 4, 16, 512), BF16),
            vmem((8, 4, 16, 512), BF16),
            vmem((16, 512), BF16),
            vmem((16, 512), BF16),
            vmem((512, 256), F32),
            vmem((512, 256), BF16),
            vmem((4, 128, 256), BF16),
            vmem((4, 8, 128), F32),
            vmem((4, 8, 128), F32),
            vmem((8, 8, 128), F32),
            vmem((4, 8, 128), F32),
            vmem((8, 8, 128), F32),
            dma((3,)), dma((3,)), dma((3,)), dma((8,)), dma((8,)), dma((32,)), dma((32,)),
            dma((NCHUNK,)), dma((NCHUNK,)),
            dma, dma, dma((12,)), dma((12,)), dma((11,)), dma((11,)),
            dma((4,)), dma((4,)), dma((4,)), dma((4,)),
            dma((8,)), dma((8,)), dma((4,)), dma((4,)), dma((8,)), dma((8,)),
        ],
        compiler_params=pltpu.CompilerParams(
            collective_id=0, has_side_effects=True, vmem_limit_bytes=60 * 2**20
        ),
        name="trace_scores",
    )(queries, keys, values, w_in, w_out.T, step_pos.reshape(1, 256), step_attr.reshape(1, 256))
    return attended, logits.T


def solution(mesh):
    in_specs = (
        P("ctx", "head"),
        P("ctx", "head"),
        P("ctx", "head"),
        P("head", "ctx"),
        P("ctx", None),
        P(),
        P(),
    )
    out_specs = (P("ctx", "head"), P())
    return jax.shard_map(body, mesh=mesh, in_specs=in_specs, out_specs=out_specs, check_vma=False)
```

```python
import functools
import math

import jax
import jax.numpy as jnp
from jax import lax
from jax.experimental import pallas as pl
from jax.experimental.pallas import tpu as pltpu
from jax.sharding import PartitionSpec as P

HD = 128
GROUP = 8
ROWS = 256
HID = 4096
CAP = 8
FEAT = 4096
NORM_EPS = 1e-06
SCALE = HD ** -0.5 * math.log2(math.e)
HIDE = -1e30
MESH = pl.DeviceIdType.MESH
F32 = jnp.float32
BF16 = jnp.bfloat16

CHUNKS = (
    ((0, 0), (1, 0), (-1, 0), (0, 1)),
    ((0, -1), (2, 0), (-2, 0), (1, 1)),
    ((1, -1), (-1, 1), (-1, -1), (3, 0)),
    ((-3, 0), (2, 1), (2, -1), (-2, 1)),
    ((-2, -1), (4, 0), (3, 1), (3, -1)),
    ((-3, 1), (-3, -1), (4, 1), (4, -1)),
    ((0, 2), (1, 2), (-1, 2), (2, 2)),
    ((-2, 2), (3, 2), (-3, 2), (4, 2)),
)
PLACE = {spot: (n, j) for n, chunk in enumerate(CHUNKS) for j, spot in enumerate(chunk)}
DZ_ORDER = (0, 1, -1, 2, -2, 3, -3, 4)
TILES = GROUP
NCHUNK = len(CHUNKS)


def coords():
    ctx = lax.axis_index("ctx")
    head = lax.axis_index("head")
    return ctx // 8, (ctx // 2) % 4, ctx % 2, head // 2, head % 2


def device(z, y, x_hi, x_lo, core):
    return ((z * 4 + y) * 2 + x_hi, x_lo * 2 + core)


EVENT = (0, 0, 0, 3, 5, 8, 10, 13)
SPLIT = (14, 18, 21, 24, 29, 32)


def fused_kernel(
    q_ref, k_ref, v_ref, w_ref, w_out_ref, pos_ref, attr_ref,
    o_ref, logit_ref,
    stage, v_in, kv, q_raw, q_t, acc, top, scores, tops, o_role, bias,
    qs_t, s_scores, s_acc, s_top, w_v,
    block, other, fa, fb, own_a, own_b, part, part16, got, square, got_sq, r1, r2, r3,
    load, swap_s, swap_r, z_s, z_r, y_s, y_r, sib_s, sib_r,
    x_s, x_r, a_s, a_r, b_s, b_r, h_s, h_r, g_s, g_r, s1, t1, s2, t2, s3, t3,
):
    z, y, x_hi, x_lo, core = coords()
    ctx = lax.axis_index("ctx")
    head = lax.axis_index("head")
    me8 = x_hi * 4 + head
    stays = x_hi == core
    sib_dev = device(z, y, x_hi, x_lo, 1 - core)

    def z_at(step):
        return device((z + step) % 8, y, x_hi, x_lo, core)

    def y_at(step):
        return device(z, (y + step) % 4, x_hi, x_lo, core)

    def chip_at(step):
        other8 = (me8 + step) % 8
        return ((z * 4 + y) * 2 + other8 // 4, other8 % 4)

    def flip_at(z_step, y_step):
        return device((z + z_step) % 8, (y + y_step) % 4, core, x_lo, x_hi)

    swap_dev = flip_at(0, 0)
    z_dev = {1: z_at(1), -1: z_at(7)}
    y_dev = {1: y_at(1), -1: y_at(3)}

    barrier = pltpu.get_barrier_semaphore()

    def greet(target):
        pl.semaphore_signal(barrier, inc=1, device_id=target, device_id_type=MESH)

    for step in range(1, 8):
        greet(chip_at(step))
    for step in (1, -1):
        greet(z_dev[step])
        greet(y_dev[step])

    def greet_far():
        for step in range(1, 8):
            if step not in (1, 7):
                greet(z_at(step))
            greet(flip_at(step, 0))
        for step in range(1, 4):
            if step == 2:
                greet(y_at(step))
            greet(flip_at(0, step))

    get_k = pltpu.make_async_copy(k_ref, stage.at[pl.ds(0, 256)], load.at[0])
    get_v = pltpu.make_async_copy(v_ref, v_in, load.at[1])
    get_w = pltpu.make_async_copy(w_ref, w_v, load.at[2])
    get_v.start()
    get_k.start()
    get_w.start()

    role = (z * 4 + y) * 2 + core
    for n, chunk in enumerate(CHUNKS):
        for j, (dz, dy) in enumerate(chunk):
            for own in range(2):
                from_core = core if own == 0 else 1 - core
                origin = (((z + 8 - dz) % 8) * 4 + (y + 4 - dy) % 4) * 2 + from_core
                bias[n * 8 + own * 4 + j] = jnp.where(origin < role, 0.0, HIDE).astype(F32)

    get_v.wait()
    v32 = v_in[...].astype(F32)
    stage[256:384, :] = v32[0:128, :].T.astype(BF16)
    stage[384:512, :] = v32[128:256, :].T.astype(BF16)
    get_k.wait()

    pl.semaphore_wait(barrier, 11)

    def spot_ref(dz, dy):
        n, j = PLACE[(dz, dy)]
        return kv.at[n, 0, j]

    def remote(src, dst, send, recv, target):
        return pltpu.make_async_remote_copy(
            src_ref=src, dst_ref=dst, send_sem=send, recv_sem=recv,
            device_id=target, device_id_type=MESH,
        )

    def start_flip(src, dst, send, recv):
        @pl.when(stays)
        def _():
            pltpu.make_async_copy(src, dst, recv).start()

        @pl.when(jnp.logical_not(stays))
        def _():
            remote(src, dst, send, recv, swap_dev).start()

    def wait_flip(src, dst, send, recv):
        @pl.when(stays)
        def _():
            pltpu.make_async_copy(src, dst, recv).wait()

        @pl.when(jnp.logical_not(stays))
        def _():
            remote(src, dst, send, recv, swap_dev).wait()

    kv_flip = (stage, spot_ref(0, 0), swap_s.at[0], swap_r.at[0])
    q_flip = (q_ref, q_raw, swap_s.at[1], swap_r.at[1])
    o_flip = (o_role, o_ref, swap_s.at[2], swap_r.at[2])
    start_flip(*kv_flip)

    Z_INDEX = {1: 0, -1: 1, 2: 2, -2: 3, 3: 4, -3: 5}

    def z_copy(dz, half=None):
        step = 1 if (dz > 0 and half != 1) else -1
        if dz == 4:
            source = spot_ref(3 if half == 0 else -3, 0).at[pl.ds(half * 256, 256)]
            target = spot_ref(4, 0).at[pl.ds(half * 256, 256)]
            at = 6 + half
        else:
            source = spot_ref(dz - step, 0)
            target = spot_ref(dz, 0)
            at = Z_INDEX[dz]
        return remote(source, target, z_s.at[at], z_r.at[at], z_dev[step])

    def y_copy(dz, dy, half=None):
        base = DZ_ORDER.index(dz) * 4
        if dy == 2:
            step = 1 if half == 0 else -1
            source = spot_ref(dz, step).at[pl.ds(half * 256, 256)]
            target = spot_ref(dz, 2).at[pl.ds(half * 256, 256)]
            at = base + 2 + half
        else:
            step = dy
            source = spot_ref(dz, 0)
            target = spot_ref(dz, dy)
            at = base + (0 if dy == 1 else 1)
        return remote(source, target, y_s.at[at], y_r.at[at], y_dev[step])

    def sib_copy(n):
        return remote(kv.at[n, 0], kv.at[n, 1], sib_s.at[n], sib_r.at[n], sib_dev)

    def arrived(dz, dy):
        if (dz, dy) == (0, 0):
            pass
        elif dy == 0 and dz == 4:
            z_copy(4, 0).wait_recv()
            z_copy(4, 1).wait_recv()
        elif dy == 0:
            z_copy(dz).wait_recv()
        elif dy == 2:
            y_copy(dz, 2, 0).wait_recv()
            y_copy(dz, 2, 1).wait_recv()
        else:
            y_copy(dz, dy).wait_recv()
        if dy == 0:
            if dz == 0:
                z_copy(1).start()
                z_copy(-1).start()
            elif abs(dz) < 3:
                z_copy(dz + (1 if dz > 0 else -1)).start()
            elif dz == 3:
                z_copy(4, 0).start()
            elif dz == -3:
                z_copy(4, 1).start()
            y_copy(dz, 1).start()
            y_copy(dz, -1).start()
        elif dy == 1:
            y_copy(dz, 2, 0).start()
        elif dy == -1:
            y_copy(dz, 2, 1).start()

    def gather_chunk(n):
        for dz, dy in CHUNKS[n]:
            if (dz, dy) != (0, 0):
                arrived(dz, dy)
        sib_copy(n).start()

    wait_flip(*kv_flip)
    arrived(0, 0)
    start_flip(*q_flip)

    pos = pos_ref[...]
    col = jnp.broadcast_to(pos.astype(F32), (128, 256)).T[:, 0:1].astype(jnp.int32)
    owner = pos // ROWS
    first = jnp.sum((col < owner * ROWS).astype(jnp.int32), axis=0, keepdims=True)
    rank = lax.broadcasted_iota(jnp.int32, (1, 256), 1) - first
    owner_col = col // ROWS
    first_col = jnp.sum((pos < owner_col * ROWS).astype(jnp.int32), axis=1, keepdims=True)
    rank_col = lax.broadcasted_iota(jnp.int32, (256, 1), 0) - first_col
    lane = lax.broadcasted_iota(jnp.int32, (256, 128), 1)
    held = (owner_col == role) & (rank_col == lane % CAP)
    s_row = jnp.sum(jnp.where(held, col - role * ROWS, 0), axis=0, keepdims=True)
    mine = (owner == role) & (rank == lax.broadcasted_iota(jnp.int32, (16, 256), 0))
    place = col - role * ROWS == lax.broadcasted_iota(jnp.int32, (256, 256), 1)
    pick = jnp.dot(mine.astype(F32).astype(BF16), place.astype(F32).astype(BF16), preferred_element_type=F32)
    pick = pick.astype(BF16)

    gather_chunk(0)
    wait_flip(*q_flip)

    def turn(t, carry):
        at = pl.multiple_of(t * HD, HD)
        q_t[t] = q_raw[:, pl.ds(at, HD)].astype(F32).T.astype(BF16)
        return carry

    lax.fori_loop(0, TILES, turn, 0, unroll=True)
    s_rows = jnp.dot(pick, q_raw[...], preferred_element_type=F32)
    stacked = [s_rows[0:8, h * HD:(h + 1) * HD] for h in range(GROUP)]
    stacked = jnp.concatenate(stacked + [jnp.zeros((64, HD), F32)], axis=0)
    qs_t[...] = stacked.T.astype(BF16)

    own_k = kv.at[0, 0, 0]

    def values_of(ref):
        return jnp.concatenate([ref[256:384, :], ref[384:512, :]], axis=1)

    def first_block(q, last):
        width = q.shape[1]
        s = jnp.dot(own_k[0:256, :], q, preferred_element_type=F32)
        key = lax.broadcasted_iota(jnp.int32, (256, width), 0)
        s = jnp.where(key <= last, s * SCALE, HIDE)
        best = jnp.max(s, axis=0, keepdims=True)
        p = jnp.exp2(s - best).astype(BF16)
        left = jnp.concatenate([values_of(own_k), jnp.ones((16, 256), BF16)], axis=0)
        return jnp.dot(left, p, preferred_element_type=F32), jnp.broadcast_to(best, (8, width))

    def diagonal(t, carry):
        query = lax.broadcasted_iota(jnp.int32, (256, 256), 1)
        acc[t], top[t] = first_block(q_t[t], query)
        return carry

    s_acc[...], s_top[...] = first_block(qs_t[...], s_row)
    gather_chunk(1)
    lax.fori_loop(0, TILES, diagonal, 0, unroll=2)

    def keys_of(n):
        return kv[n, :, :, 0:256, :].reshape(2048, HD)

    def best_of(s, n):
        best = None
        for at in range(8):
            part_best = jnp.max(s[at * 256:(at + 1) * 256].reshape(32, 8, s.shape[1]), axis=0) + bias[n * 8 + at]
            best = part_best if best is None else jnp.maximum(best, part_best)
        return best

    def mix(n, s_of, row):
        pieces = []
        left = []
        for at in range(8):
            shift = row - bias[n * 8 + at]
            pieces.append(jnp.exp2(s_of(at) * SCALE - shift).astype(BF16))
            left.append(kv[n, at // 4, at % 4, 256:384, :])
            left.append(kv[n, at // 4, at % 4, 384:512, :])
        left = jnp.concatenate(left, axis=1)
        left = jnp.concatenate([left, jnp.ones((16, 2048), BF16)], axis=0)
        return jnp.dot(left, jnp.concatenate(pieces, axis=0), preferred_element_type=F32)

    def score(n, t, slot):
        s = jnp.dot(keys_of(n), q_t[t], preferred_element_type=F32)
        scores[slot] = s
        tops[slot] = best_of(s, n)

    def absorb(n, t, slot):
        old = top[t]
        new = jnp.maximum(old, jnp.max(tops[slot], axis=0, keepdims=True) * SCALE)
        top[t] = new
        fade = jnp.exp2(old - new)[:1]
        update = mix(n, lambda at: scores[slot, at * 256:(at + 1) * 256, :], new[:1])
        acc[t] = acc[t] * fade + update

    def step_rows(n):
        s = jnp.dot(keys_of(n), qs_t[...], preferred_element_type=F32)
        s_scores[...] = s
        old = s_top[...]
        new = jnp.maximum(old, jnp.max(best_of(s, n), axis=0, keepdims=True) * SCALE)
        s_top[...] = new
        fade = jnp.exp2(old - new)[:1]
        update = mix(n, lambda at: s_scores[at * 256:(at + 1) * 256, :], new[:1])
        s_acc[...] = s_acc[...] * fade + update

    def pair(step, carry):
        n = step // 4
        t = (step % 4) * 2
        score(n, t + 1, 1)
        absorb(n, t, 0)
        follow = jnp.minimum(step + 1, NCHUNK * 4 - 1)
        score(follow // 4, (follow % 4) * 2, 0)
        absorb(n, t + 1, 1)
        return carry

    def turn_a(step, carry):
        for m in range(2, NCHUNK):
            @pl.when(step == EVENT[m])
            def _():
                gather_chunk(m)
                if m == 6:
                    greet_far()

        due = jnp.int32(1)
        fresh = step == EVENT[2] + 1
        for m in range(2, NCHUNK):
            due = due + (step > EVENT[m]).astype(jnp.int32)
            fresh = fresh | (step == EVENT[m] + 1)

        @pl.when(fresh)
        def _():
            remote(kv.at[due, 0], kv.at[due, 1], sib_s.at[due], sib_r.at[due], sib_dev).wait_recv()
            step_rows(due)

        return pair(step, carry)

    sib_copy(0).wait_recv()
    step_rows(0)
    sib_copy(1).wait_recv()
    step_rows(1)
    score(0, 0, 0)
    lax.fori_loop(0, SPLIT[0], turn_a, 0)
    sib_copy(7).wait_recv()
    step_rows(7)

    done = s_acc[...]
    mixed = (done[0:128, :] / done[128:129, :]).T
    row8 = jnp.concatenate([mixed[h * 8:(h + 1) * 8, :] for h in range(GROUP)], axis=1)
    row16 = jnp.concatenate([row8, row8], axis=0)
    row_id = lax.broadcasted_iota(jnp.int32, (16, 1024), 0)
    block[...] = jnp.where(row_id // CAP == core, row16, 0.0).astype(BF16)
    pair_up = remote(block, other, x_s, x_r, sib_dev)
    pair_up.start()
    pair_up.wait()
    both = block[...] + other[...]
    own_a[...] = both[:, :512]
    own_b[...] = both[:, 512:]

    def copy_a(index, src, dst, target):
        return remote(src, dst, a_s.at[index], a_r.at[index], target)

    def copy_b(index, src, dst, target):
        return remote(src, dst, b_s.at[index], b_r.at[index], target)

    flip_b = (own_b, fb.at[0, 0], b_s.at[0], b_r.at[0])
    flip_a = (own_a, fa.at[0, 0], a_s.at[0], a_r.at[0])
    b_z = [copy_b(k, own_b, fb.at[k, 0], flip_at(k, 0)) for k in range(1, 8)]
    a_y = [copy_a(k, own_a, fa.at[0, k], flip_at(0, k)) for k in range(1, 4)]
    pl.semaphore_wait(barrier, 16)
    start_flip(*flip_a)
    start_flip(*flip_b)
    for c in a_y + b_z:
        c.start()

    low, high = pl.ds(0, 2), pl.ds(2, 2)
    a_z = [copy_a(3 + k, fa.at[0], fa.at[d % 8], z_at(d % 8)) for k, d in ((1, 1), (2, -1), (3, 2), (4, -2))]
    a_far = [
        copy_a(8, fa.at[2], fa.at[3], z_at(1)),
        copy_a(9, fa.at[6], fa.at[5], z_at(7)),
        copy_a(10, fa.at[2, low], fa.at[4, low], z_at(2)),
        copy_a(11, fa.at[6, high], fa.at[4, high], z_at(6)),
    ]
    b_y = [copy_b(7 + k, fb.at[:, 0], fb.at[:, k], y_at(k)) for k in (1, 3, 2)]

    lax.fori_loop(SPLIT[0], SPLIT[1], pair, 0)
    wait_flip(*flip_a)
    for c in a_y:
        c.wait_recv()
    for c in a_z:
        c.start()
    lax.fori_loop(SPLIT[1], SPLIT[2], pair, 0)
    wait_flip(*flip_b)
    for c in b_z:
        c.wait_recv()
    for c in b_y:
        c.start()
    lax.fori_loop(SPLIT[2], SPLIT[3], pair, 0)

    def finish(t, carry):
        at = pl.multiple_of(t * HD, HD)
        total = acc[t]
        o_role[:, pl.ds(at, HD)] = (total[0:128, :] / total[128:129, :]).T.astype(BF16)
        return carry

    for c in a_z:
        c.wait_recv()
    for c in a_far:
        c.start()
    lax.fori_loop(SPLIT[3], SPLIT[4], pair, 0)

    r = lax.broadcasted_iota(jnp.int32, (128, 256), 0)
    dz = head * 2 + r // 64
    zz = (z + 8 - dz) % 8
    yy = (y + 4 - (r // 16) % 4) % 4
    slot = ((zz * 4 + yy) * 2 + (r // 8) % 2) * CAP + r % CAP
    match = slot == owner * CAP + rank
    match32 = match.astype(F32)
    wanted = jnp.sum(jnp.where(match, (attr_ref[...] == ctx // 16).astype(F32), 0.0), axis=1, keepdims=True)

    w32 = w_out_ref[...].astype(F32)
    odd = lax.broadcasted_iota(jnp.int32, (16, 256), 0) % 2 == 1
    w16 = jnp.where(odd, w32[1:2, :], w32[0:1, :]).astype(BF16)
    get_w.wait()
    for c in b_y + a_far:
        c.wait_recv()

    half_a = fa[...].reshape(512, 512)
    half_b = fb[...].reshape(512, 512)
    partial = jnp.dot(half_a, w_v[0:512, :], preferred_element_type=F32)
    partial = partial + jnp.dot(half_b, w_v[512:1024, :], preferred_element_type=F32)
    part[...] = partial
    part16[...] = partial.astype(BF16)
    for j in range(4):
        summed = jnp.zeros((128, 128), F32)
        for half in (fa, fb):
            rows32 = half[2 * j:2 * j + 2].reshape(128, 512).astype(F32)
            sq = rows32 * rows32
            for c in range(4):
                summed = summed + sq[:, c * 128:(c + 1) * 128]
        total = jnp.broadcast_to(jnp.sum(summed, axis=1, keepdims=True), (128, 128))
        square[j] = total.T[0:8, :]

    def head_dev(step):
        return (ctx, (head + step) % 4)

    sends = []
    for step in range(1, 4):
        to = (head + step) % 4
        at = pl.ds(pl.multiple_of(to * 128, 128), 128)
        sends.append(remote(square.at[to], got_sq.at[step], g_s.at[step], g_r.at[step], head_dev(step)))
        sends.append(remote(part16.at[at], got.at[step], h_s.at[step], h_r.at[step], head_dev(step)))
    for c in sends:
        c.start()
    lax.fori_loop(SPLIT[4], SPLIT[5], pair, 0)
    pre = part[pl.ds(pl.multiple_of(head * 128, 128), 128), :]
    squares = square[head]
    for c in sends:
        c.wait()
    for step in range(1, 4):
        pre = pre + got[step].astype(F32)
        squares = squares + got_sq[step]
    factor = lax.rsqrt(squares[0:1, :] / FEAT + NORM_EPS)
    factor = jnp.broadcast_to(factor, (128, 128)).T[:, 0:1]
    hidden = jnp.where(wanted > 0.5, jnp.maximum(pre * factor, 0.0), 0.0).astype(BF16)
    terms = lax.dot_general(w16, hidden, (((1,), (1,)), ((), ())), preferred_element_type=F32)[0:8, :]
    mapped = jnp.dot(terms, match32, preferred_element_type=F32, precision=lax.Precision.HIGHEST)
    line = lax.broadcasted_iota(jnp.int32, (8, 128), 0)
    tile = jnp.where(line < 2, mapped[:, :128], mapped[:, 128:])

    def all_sum(value, buf, send, recv, me, count, at, beside=None):
        buf[me] = value
        copies = []
        for step in range(1, count):
            copies.append(remote(buf.at[me], buf.at[me], send.at[step], recv.at[step], at(step)))
        for c in copies:
            c.start()
        if beside is not None:
            beside()
        for c in copies:
            c.wait_recv()
        total = buf[0]
        for i in range(1, count):
            total = total + buf[i]
        return total, copies

    def hand_back():
        lax.fori_loop(0, TILES, finish, 0, unroll=2)
        start_flip(*o_flip)

    tile, c1 = all_sum(tile, r1, s1, t1, me8, 8, chip_at, hand_back)
    tile, c2 = all_sum(tile, r2, s2, t2, y, 4, y_at)
    tile, c3 = all_sum(tile, r3, s3, t3, z, 8, z_at)
    logit_ref[:, 0:128] = tile[0:2, :]
    logit_ref[:, 128:256] = tile[2:4, :]

    for c in c1 + c2 + c3 + a_y + a_z + a_far + b_z + b_y:
        c.wait_send()
    for dz in DZ_ORDER:
        if dz == 4:
            z_copy(4, 0).wait_send()
            z_copy(4, 1).wait_send()
        elif dz != 0:
            z_copy(dz).wait_send()
        y_copy(dz, 1).wait_send()
        y_copy(dz, -1).wait_send()
        y_copy(dz, 2, 0).wait_send()
        y_copy(dz, 2, 1).wait_send()
    for n in range(NCHUNK):
        sib_copy(n).wait_send()
    wait_flip(*o_flip)


def body(queries, keys, values, w_in, w_out, step_pos, step_attr):
    dma = pltpu.SemaphoreType.DMA
    vmem = pltpu.VMEM
    here = pl.BlockSpec(memory_space=pltpu.VMEM)
    away = pl.BlockSpec(memory_space=pl.ANY)
    attended, logits = pl.pallas_call(
        fused_kernel,
        out_shape=(
            jax.ShapeDtypeStruct(queries.shape, BF16),
            jax.ShapeDtypeStruct((2, 256), F32),
        ),
        in_specs=[away] * 4 + [here] * 3,
        out_specs=(here, here),
        scratch_shapes=[
            vmem((512, HD), BF16),
            vmem((ROWS, HD), BF16),
            vmem((NCHUNK, 2, 4, 512, HD), BF16),
            vmem((ROWS, GROUP * HD), BF16),
            vmem((TILES, HD, 256), BF16),
            vmem((TILES, 144, 256), F32),
            vmem((TILES, 8, 256), F32),
            vmem((2, 2048, 256), F32),
            vmem((2, 8, 256), F32),
            vmem((ROWS, GROUP * HD), BF16),
            pltpu.SMEM((64,), F32),
            vmem((HD, 128), BF16),
            vmem((2048, 128), F32),
            vmem((144, 128), F32),
            vmem((8, 128), F32),
            vmem((1024, 256), BF16),
            vmem((16, 1024), BF16),
            vmem((16, 1024), BF16),
            vmem((8, 4, 16, 512), BF16),
            vmem((8, 4, 16, 512), BF16),
            vmem((16, 512), BF16),
            vmem((16, 512), BF16),
            vmem((512, 256), F32),
            vmem((512, 256), BF16),
            vmem((4, 128, 256), BF16),
            vmem((4, 8, 128), F32),
            vmem((4, 8, 128), F32),
            vmem((8, 8, 128), F32),
            vmem((4, 8, 128), F32),
            vmem((8, 8, 128), F32),
            dma((3,)), dma((3,)), dma((3,)), dma((8,)), dma((8,)), dma((32,)), dma((32,)),
            dma((NCHUNK,)), dma((NCHUNK,)),
            dma, dma, dma((12,)), dma((12,)), dma((11,)), dma((11,)),
            dma((4,)), dma((4,)), dma((4,)), dma((4,)),
            dma((8,)), dma((8,)), dma((4,)), dma((4,)), dma((8,)), dma((8,)),
        ],
        compiler_params=pltpu.CompilerParams(
            collective_id=0, has_side_effects=True, vmem_limit_bytes=60 * 2**20
        ),
        name="trace_scores",
    )(queries, keys, values, w_in, w_out.T, step_pos.reshape(1, 256), step_attr.reshape(1, 256))
    return attended, logits.T


def solution(mesh):
    in_specs = (
        P("ctx", "head"),
        P("ctx", "head"),
        P("ctx", "head"),
        P("head", "ctx"),
        P("ctx", None),
        P(),
        P(),
    )
    out_specs = (P("ctx", "head"), P())
    return jax.shard_map(body, mesh=mesh, in_specs=in_specs, out_specs=out_specs, check_vma=False)
```

```python
import functools
import math

import jax
import jax.numpy as jnp
from jax import lax
from jax.experimental import pallas as pl
from jax.experimental.pallas import tpu as pltpu
from jax.sharding import PartitionSpec as P

HD = 128
GROUP = 8
ROWS = 256
HID = 4096
CAP = 8
FEAT = 4096
NORM_EPS = 1e-06
SCALE = HD ** -0.5 * math.log2(math.e)
HIDE = -1e30
MESH = pl.DeviceIdType.MESH
F32 = jnp.float32
BF16 = jnp.bfloat16

CHUNKS = (
    ((0, 0), (1, 0), (-1, 0), (0, 1)),
    ((0, -1), (2, 0), (-2, 0), (1, 1)),
    ((1, -1), (-1, 1), (-1, -1), (3, 0)),
    ((-3, 0), (2, 1), (2, -1), (-2, 1)),
    ((-2, -1), (4, 0), (3, 1), (3, -1)),
    ((-3, 1), (-3, -1), (4, 1), (4, -1)),
    ((0, 2), (1, 2), (-1, 2), (2, 2)),
    ((-2, 2), (3, 2), (-3, 2), (4, 2)),
)
PLACE = {spot: (n, j) for n, chunk in enumerate(CHUNKS) for j, spot in enumerate(chunk)}
DZ_ORDER = (0, 1, -1, 2, -2, 3, -3, 4)
TILES = GROUP
NCHUNK = len(CHUNKS)


def coords():
    ctx = lax.axis_index("ctx")
    head = lax.axis_index("head")
    return ctx // 8, (ctx // 2) % 4, ctx % 2, head // 2, head % 2


def device(z, y, x_hi, x_lo, core):
    return ((z * 4 + y) * 2 + x_hi, x_lo * 2 + core)


EVENT = (0, 0, 0, 3, 5, 8, 10, 13)
SPLIT = (14, 17, 20, 23, 28, 32)


def fused_kernel(
    q_ref, k_ref, v_ref, w_ref, w_out_ref, pos_ref, attr_ref,
    o_ref, logit_ref,
    stage, v_in, kv, q_raw, q_t, acc, top, scores, tops, o_role, bias,
    qs_t, s_scores, s_acc, s_top, w_v,
    block, other, fa, fb, own_a, own_b, part, part16, got, square, got_sq, r1, r2, r3,
    load, swap_s, swap_r, z_s, z_r, y_s, y_r, sib_s, sib_r,
    x_s, x_r, a_s, a_r, b_s, b_r, h_s, h_r, g_s, g_r, s1, t1, s2, t2, s3, t3,
):
    z, y, x_hi, x_lo, core = coords()
    ctx = lax.axis_index("ctx")
    head = lax.axis_index("head")
    me8 = x_hi * 4 + head
    stays = x_hi == core
    sib_dev = device(z, y, x_hi, x_lo, 1 - core)

    def z_at(step):
        return device((z + step) % 8, y, x_hi, x_lo, core)

    def y_at(step):
        return device(z, (y + step) % 4, x_hi, x_lo, core)

    def chip_at(step):
        other8 = (me8 + step) % 8
        return ((z * 4 + y) * 2 + other8 // 4, other8 % 4)

    def flip_at(z_step, y_step):
        return device((z + z_step) % 8, (y + y_step) % 4, core, x_lo, x_hi)

    swap_dev = flip_at(0, 0)
    z_dev = {1: z_at(1), -1: z_at(7)}
    y_dev = {1: y_at(1), -1: y_at(3)}

    barrier = pltpu.get_barrier_semaphore()

    def greet(target):
        pl.semaphore_signal(barrier, inc=1, device_id=target, device_id_type=MESH)

    for step in range(1, 8):
        greet(chip_at(step))
    for step in (1, -1):
        greet(z_dev[step])
        greet(y_dev[step])

    def greet_far():
        for step in range(1, 8):
            if step not in (1, 7):
                greet(z_at(step))
            greet(flip_at(step, 0))
        for step in range(1, 4):
            if step == 2:
                greet(y_at(step))
            greet(flip_at(0, step))

    get_k = pltpu.make_async_copy(k_ref, stage.at[pl.ds(0, 256)], load.at[0])
    get_v = pltpu.make_async_copy(v_ref, v_in, load.at[1])
    get_w = pltpu.make_async_copy(w_ref, w_v, load.at[2])
    get_v.start()
    get_k.start()
    get_w.start()

    role = (z * 4 + y) * 2 + core
    for n, chunk in enumerate(CHUNKS):
        for j, (dz, dy) in enumerate(chunk):
            for own in range(2):
                from_core = core if own == 0 else 1 - core
                origin = (((z + 8 - dz) % 8) * 4 + (y + 4 - dy) % 4) * 2 + from_core
                bias[n * 8 + own * 4 + j] = jnp.where(origin < role, 0.0, HIDE).astype(F32)

    get_v.wait()
    v32 = v_in[...].astype(F32)
    stage[256:384, :] = v32[0:128, :].T.astype(BF16)
    stage[384:512, :] = v32[128:256, :].T.astype(BF16)
    get_k.wait()

    pl.semaphore_wait(barrier, 11)

    def spot_ref(dz, dy):
        n, j = PLACE[(dz, dy)]
        return kv.at[n, 0, j]

    def remote(src, dst, send, recv, target):
        return pltpu.make_async_remote_copy(
            src_ref=src, dst_ref=dst, send_sem=send, recv_sem=recv,
            device_id=target, device_id_type=MESH,
        )

    def start_flip(src, dst, send, recv):
        @pl.when(stays)
        def _():
            pltpu.make_async_copy(src, dst, recv).start()

        @pl.when(jnp.logical_not(stays))
        def _():
            remote(src, dst, send, recv, swap_dev).start()

    def wait_flip(src, dst, send, recv):
        @pl.when(stays)
        def _():
            pltpu.make_async_copy(src, dst, recv).wait()

        @pl.when(jnp.logical_not(stays))
        def _():
            remote(src, dst, send, recv, swap_dev).wait()

    kv_flip = (stage, spot_ref(0, 0), swap_s.at[0], swap_r.at[0])
    q_flip = (q_ref, q_raw, swap_s.at[1], swap_r.at[1])
    o_flip = (o_role, o_ref, swap_s.at[2], swap_r.at[2])
    start_flip(*kv_flip)

    Z_INDEX = {1: 0, -1: 1, 2: 2, -2: 3, 3: 4, -3: 5}

    def z_copy(dz, half=None):
        step = 1 if (dz > 0 and half != 1) else -1
        if dz == 4:
            source = spot_ref(3 if half == 0 else -3, 0).at[pl.ds(half * 256, 256)]
            target = spot_ref(4, 0).at[pl.ds(half * 256, 256)]
            at = 6 + half
        else:
            source = spot_ref(dz - step, 0)
            target = spot_ref(dz, 0)
            at = Z_INDEX[dz]
        return remote(source, target, z_s.at[at], z_r.at[at], z_dev[step])

    def y_copy(dz, dy, half=None):
        base = DZ_ORDER.index(dz) * 4
        if dy == 2:
            step = 1 if half == 0 else -1
            source = spot_ref(dz, step).at[pl.ds(half * 256, 256)]
            target = spot_ref(dz, 2).at[pl.ds(half * 256, 256)]
            at = base + 2 + half
        else:
            step = dy
            source = spot_ref(dz, 0)
            target = spot_ref(dz, dy)
            at = base + (0 if dy == 1 else 1)
        return remote(source, target, y_s.at[at], y_r.at[at], y_dev[step])

    def sib_copy(n):
        return remote(kv.at[n, 0], kv.at[n, 1], sib_s.at[n], sib_r.at[n], sib_dev)

    def arrived(dz, dy):
        if (dz, dy) == (0, 0):
            pass
        elif dy == 0 and dz == 4:
            z_copy(4, 0).wait_recv()
            z_copy(4, 1).wait_recv()
        elif dy == 0:
            z_copy(dz).wait_recv()
        elif dy == 2:
            y_copy(dz, 2, 0).wait_recv()
            y_copy(dz, 2, 1).wait_recv()
        else:
            y_copy(dz, dy).wait_recv()
        if dy == 0:
            if dz == 0:
                z_copy(1).start()
                z_copy(-1).start()
            elif abs(dz) < 3:
                z_copy(dz + (1 if dz > 0 else -1)).start()
            elif dz == 3:
                z_copy(4, 0).start()
            elif dz == -3:
                z_copy(4, 1).start()
            y_copy(dz, 1).start()
            y_copy(dz, -1).start()
        elif dy == 1:
            y_copy(dz, 2, 0).start()
        elif dy == -1:
            y_copy(dz, 2, 1).start()

    def gather_chunk(n):
        for dz, dy in CHUNKS[n]:
            if (dz, dy) != (0, 0):
                arrived(dz, dy)
        sib_copy(n).start()

    wait_flip(*kv_flip)
    arrived(0, 0)
    start_flip(*q_flip)

    pos = pos_ref[...]
    col = jnp.broadcast_to(pos.astype(F32), (128, 256)).T[:, 0:1].astype(jnp.int32)
    owner = pos // ROWS
    first = jnp.sum((col < owner * ROWS).astype(jnp.int32), axis=0, keepdims=True)
    rank = lax.broadcasted_iota(jnp.int32, (1, 256), 1) - first
    owner_col = col // ROWS
    first_col = jnp.sum((pos < owner_col * ROWS).astype(jnp.int32), axis=1, keepdims=True)
    rank_col = lax.broadcasted_iota(jnp.int32, (256, 1), 0) - first_col
    lane = lax.broadcasted_iota(jnp.int32, (256, 128), 1)
    held = (owner_col == role) & (rank_col == lane % CAP)
    s_row = jnp.sum(jnp.where(held, col - role * ROWS, 0), axis=0, keepdims=True)
    mine = (owner == role) & (rank == lax.broadcasted_iota(jnp.int32, (16, 256), 0))
    place = col - role * ROWS == lax.broadcasted_iota(jnp.int32, (256, 256), 1)
    pick = jnp.dot(mine.astype(F32).astype(BF16), place.astype(F32).astype(BF16), preferred_element_type=F32)
    pick = pick.astype(BF16)

    gather_chunk(0)
    wait_flip(*q_flip)

    def turn(t, carry):
        at = pl.multiple_of(t * HD, HD)
        q_t[t] = q_raw[:, pl.ds(at, HD)].astype(F32).T.astype(BF16)
        return carry

    lax.fori_loop(0, TILES, turn, 0, unroll=True)
    s_rows = jnp.dot(pick, q_raw[...], preferred_element_type=F32)
    stacked = [s_rows[0:8, h * HD:(h + 1) * HD] for h in range(GROUP)]
    stacked = jnp.concatenate(stacked + [jnp.zeros((64, HD), F32)], axis=0)
    qs_t[...] = stacked.T.astype(BF16)

    own_k = kv.at[0, 0, 0]

    def values_of(ref):
        return jnp.concatenate([ref[256:384, :], ref[384:512, :]], axis=1)

    def first_block(q, last):
        width = q.shape[1]
        s = jnp.dot(own_k[0:256, :], q, preferred_element_type=F32)
        key = lax.broadcasted_iota(jnp.int32, (256, width), 0)
        s = jnp.where(key <= last, s * SCALE, HIDE)
        best = jnp.max(s, axis=0, keepdims=True)
        p = jnp.exp2(s - best).astype(BF16)
        left = jnp.concatenate([values_of(own_k), jnp.ones((16, 256), BF16)], axis=0)
        return jnp.dot(left, p, preferred_element_type=F32), jnp.broadcast_to(best, (8, width))

    def diagonal(t, carry):
        query = lax.broadcasted_iota(jnp.int32, (256, 256), 1)
        acc[t], top[t] = first_block(q_t[t], query)
        return carry

    s_acc[...], s_top[...] = first_block(qs_t[...], s_row)
    gather_chunk(1)
    lax.fori_loop(0, TILES, diagonal, 0, unroll=2)

    def keys_of(n):
        return kv[n, :, :, 0:256, :].reshape(2048, HD)

    def best_of(s, n):
        best = None
        for at in range(8):
            part_best = jnp.max(s[at * 256:(at + 1) * 256].reshape(32, 8, s.shape[1]), axis=0) + bias[n * 8 + at]
            best = part_best if best is None else jnp.maximum(best, part_best)
        return best

    def mix(n, s_of, row):
        pieces = []
        left = []
        for at in range(8):
            shift = row - bias[n * 8 + at]
            pieces.append(jnp.exp2(s_of(at) * SCALE - shift).astype(BF16))
            left.append(kv[n, at // 4, at % 4, 256:384, :])
            left.append(kv[n, at // 4, at % 4, 384:512, :])
        left = jnp.concatenate(left, axis=1)
        left = jnp.concatenate([left, jnp.ones((16, 2048), BF16)], axis=0)
        return jnp.dot(left, jnp.concatenate(pieces, axis=0), preferred_element_type=F32)

    def score(n, t, slot):
        s = jnp.dot(keys_of(n), q_t[t], preferred_element_type=F32)
        scores[slot] = s
        tops[slot] = best_of(s, n)

    def absorb(n, t, slot):
        old = top[t]
        new = jnp.maximum(old, jnp.max(tops[slot], axis=0, keepdims=True) * SCALE)
        top[t] = new
        fade = jnp.exp2(old - new)[:1]
        update = mix(n, lambda at: scores[slot, at * 256:(at + 1) * 256, :], new[:1])
        acc[t] = acc[t] * fade + update

    def in_sight(n):
        seen = n < 0
        for m, chunk in enumerate(CHUNKS):
            for dz in sorted({spot[0] for spot in chunk}):
                seen = seen | ((n == m) & ((z + 8 - dz) % 8 <= z))
        return seen

    def step_rows(n):
        @pl.when(in_sight(jnp.int32(n)))
        def _():
            s = jnp.dot(keys_of(n), qs_t[...], preferred_element_type=F32)
            s_scores[...] = s
            old = s_top[...]
            new = jnp.maximum(old, jnp.max(best_of(s, n), axis=0, keepdims=True) * SCALE)
            s_top[...] = new
            fade = jnp.exp2(old - new)[:1]
            update = mix(n, lambda at: s_scores[at * 256:(at + 1) * 256, :], new[:1])
            s_acc[...] = s_acc[...] * fade + update

    def pair(step, carry):
        n = step // 4
        t = (step % 4) * 2
        score(n, t + 1, 1)
        absorb(n, t, 0)
        follow = jnp.minimum(step + 1, NCHUNK * 4 - 1)
        score(follow // 4, (follow % 4) * 2, 0)
        absorb(n, t + 1, 1)
        return carry

    def turn_a(step, carry):
        for m in range(2, NCHUNK):
            @pl.when(step == EVENT[m])
            def _():
                gather_chunk(m)
                if m == 6:
                    greet_far()

        due = jnp.int32(1)
        fresh = step == EVENT[2] + 1
        for m in range(2, NCHUNK):
            due = due + (step > EVENT[m]).astype(jnp.int32)
            fresh = fresh | (step == EVENT[m] + 1)

        @pl.when(fresh)
        def _():
            remote(kv.at[due, 0], kv.at[due, 1], sib_s.at[due], sib_r.at[due], sib_dev).wait_recv()
            step_rows(due)

        return pair(step, carry)

    sib_copy(0).wait_recv()
    step_rows(0)
    sib_copy(1).wait_recv()
    step_rows(1)
    score(0, 0, 0)
    lax.fori_loop(0, SPLIT[0], turn_a, 0)
    sib_copy(7).wait_recv()
    step_rows(7)

    done = s_acc[...]
    mixed = (done[0:128, :] / done[128:129, :]).T
    row8 = jnp.concatenate([mixed[h * 8:(h + 1) * 8, :] for h in range(GROUP)], axis=1)
    row16 = jnp.concatenate([row8, row8], axis=0)
    row_id = lax.broadcasted_iota(jnp.int32, (16, 1024), 0)
    block[...] = jnp.where(row_id // CAP == core, row16, 0.0).astype(BF16)
    pair_up = remote(block, other, x_s, x_r, sib_dev)
    pair_up.start()
    pair_up.wait()
    both = block[...] + other[...]
    own_a[...] = both[:, :512]
    own_b[...] = both[:, 512:]

    def copy_a(index, src, dst, target):
        return remote(src, dst, a_s.at[index], a_r.at[index], target)

    def copy_b(index, src, dst, target):
        return remote(src, dst, b_s.at[index], b_r.at[index], target)

    flip_b = (own_b, fb.at[0, 0], b_s.at[0], b_r.at[0])
    flip_a = (own_a, fa.at[0, 0], a_s.at[0], a_r.at[0])
    b_z = [copy_b(k, own_b, fb.at[k, 0], flip_at(k, 0)) for k in range(1, 8)]
    a_y = [copy_a(k, own_a, fa.at[0, k], flip_at(0, k)) for k in range(1, 4)]
    pl.semaphore_wait(barrier, 16)
    start_flip(*flip_a)
    start_flip(*flip_b)
    for c in a_y + b_z:
        c.start()

    low, high = pl.ds(0, 2), pl.ds(2, 2)
    a_z = [copy_a(3 + k, fa.at[0], fa.at[d % 8], z_at(d % 8)) for k, d in ((1, 1), (2, -1), (3, 2), (4, -2))]
    a_far = [
        copy_a(8, fa.at[2], fa.at[3], z_at(1)),
        copy_a(9, fa.at[6], fa.at[5], z_at(7)),
        copy_a(10, fa.at[2, low], fa.at[4, low], z_at(2)),
        copy_a(11, fa.at[6, high], fa.at[4, high], z_at(6)),
    ]
    b_y = [copy_b(7 + k, fb.at[:, 0], fb.at[:, k], y_at(k)) for k in (1, 3, 2)]

    lax.fori_loop(SPLIT[0], SPLIT[1], pair, 0)
    wait_flip(*flip_a)
    for c in a_y:
        c.wait_recv()
    for c in a_z:
        c.start()
    lax.fori_loop(SPLIT[1], SPLIT[2], pair, 0)
    wait_flip(*flip_b)
    for c in b_z:
        c.wait_recv()
    for c in b_y:
        c.start()
    lax.fori_loop(SPLIT[2], SPLIT[3], pair, 0)

    def finish(t, carry):
        at = pl.multiple_of(t * HD, HD)
        total = acc[t]
        o_role[:, pl.ds(at, HD)] = (total[0:128, :] / total[128:129, :]).T.astype(BF16)
        return carry

    for c in a_z:
        c.wait_recv()
    for c in a_far:
        c.start()
    lax.fori_loop(SPLIT[3], SPLIT[4], pair, 0)

    r = lax.broadcasted_iota(jnp.int32, (128, 256), 0)
    dz = head * 2 + r // 64
    zz = (z + 8 - dz) % 8
    yy = (y + 4 - (r // 16) % 4) % 4
    slot = ((zz * 4 + yy) * 2 + (r // 8) % 2) * CAP + r % CAP
    match = slot == owner * CAP + rank
    match32 = match.astype(F32)
    wanted = jnp.sum(jnp.where(match, (attr_ref[...] == ctx // 16).astype(F32), 0.0), axis=1, keepdims=True)

    w32 = w_out_ref[...].astype(F32)
    odd = lax.broadcasted_iota(jnp.int32, (16, 256), 0) % 2 == 1
    w16 = jnp.where(odd, w32[1:2, :], w32[0:1, :]).astype(BF16)
    get_w.wait()
    for c in b_y + a_far:
        c.wait_recv()

    half_a = fa[...].reshape(512, 512)
    half_b = fb[...].reshape(512, 512)
    partial = jnp.dot(half_a, w_v[0:512, :], preferred_element_type=F32)
    partial = partial + jnp.dot(half_b, w_v[512:1024, :], preferred_element_type=F32)
    part[...] = partial
    part16[...] = partial.astype(BF16)
    for j in range(4):
        summed = jnp.zeros((128, 128), F32)
        for half in (fa, fb):
            rows32 = half[2 * j:2 * j + 2].reshape(128, 512).astype(F32)
            sq = rows32 * rows32
            for c in range(4):
                summed = summed + sq[:, c * 128:(c + 1) * 128]
        total = jnp.broadcast_to(jnp.sum(summed, axis=1, keepdims=True), (128, 128))
        square[j] = total.T[0:8, :]

    def head_dev(step):
        return (ctx, (head + step) % 4)

    sends = []
    for step in range(1, 4):
        to = (head + step) % 4
        at = pl.ds(pl.multiple_of(to * 128, 128), 128)
        sends.append(remote(square.at[to], got_sq.at[step], g_s.at[step], g_r.at[step], head_dev(step)))
        sends.append(remote(part16.at[at], got.at[step], h_s.at[step], h_r.at[step], head_dev(step)))
    for c in sends:
        c.start()
    lax.fori_loop(SPLIT[4], SPLIT[5], pair, 0)
    pre = part[pl.ds(pl.multiple_of(head * 128, 128), 128), :]
    squares = square[head]
    for c in sends:
        c.wait()
    for step in range(1, 4):
        pre = pre + got[step].astype(F32)
        squares = squares + got_sq[step]
    factor = lax.rsqrt(squares[0:1, :] / FEAT + NORM_EPS)
    factor = jnp.broadcast_to(factor, (128, 128)).T[:, 0:1]
    hidden = jnp.where(wanted > 0.5, jnp.maximum(pre * factor, 0.0), 0.0).astype(BF16)
    terms = lax.dot_general(w16, hidden, (((1,), (1,)), ((), ())), preferred_element_type=F32)[0:8, :]
    mapped = jnp.dot(terms, match32, preferred_element_type=F32, precision=lax.Precision.HIGHEST)
    line = lax.broadcasted_iota(jnp.int32, (8, 128), 0)
    tile = jnp.where(line < 2, mapped[:, :128], mapped[:, 128:])

    def all_sum(value, buf, send, recv, me, count, at, beside=None):
        buf[me] = value
        copies = []
        for step in range(1, count):
            copies.append(remote(buf.at[me], buf.at[me], send.at[step], recv.at[step], at(step)))
        for c in copies:
            c.start()
        if beside is not None:
            beside()
        for c in copies:
            c.wait_recv()
        total = buf[0]
        for i in range(1, count):
            total = total + buf[i]
        return total, copies

    def hand_back():
        lax.fori_loop(0, TILES, finish, 0, unroll=2)
        start_flip(*o_flip)

    tile, c1 = all_sum(tile, r1, s1, t1, me8, 8, chip_at, hand_back)
    tile, c2 = all_sum(tile, r2, s2, t2, y, 4, y_at)
    tile, c3 = all_sum(tile, r3, s3, t3, z, 8, z_at)
    logit_ref[:, 0:128] = tile[0:2, :]
    logit_ref[:, 128:256] = tile[2:4, :]

    for c in c1 + c2 + c3 + a_y + a_z + a_far + b_z + b_y:
        c.wait_send()
    for dz in DZ_ORDER:
        if dz == 4:
            z_copy(4, 0).wait_send()
            z_copy(4, 1).wait_send()
        elif dz != 0:
            z_copy(dz).wait_send()
        y_copy(dz, 1).wait_send()
        y_copy(dz, -1).wait_send()
        y_copy(dz, 2, 0).wait_send()
        y_copy(dz, 2, 1).wait_send()
    for n in range(NCHUNK):
        sib_copy(n).wait_send()
    wait_flip(*o_flip)


def body(queries, keys, values, w_in, w_out, step_pos, step_attr):
    dma = pltpu.SemaphoreType.DMA
    vmem = pltpu.VMEM
    here = pl.BlockSpec(memory_space=pltpu.VMEM)
    away = pl.BlockSpec(memory_space=pl.ANY)
    attended, logits = pl.pallas_call(
        fused_kernel,
        out_shape=(
            jax.ShapeDtypeStruct(queries.shape, BF16),
            jax.ShapeDtypeStruct((2, 256), F32),
        ),
        in_specs=[away] * 4 + [here] * 3,
        out_specs=(here, here),
        scratch_shapes=[
            vmem((512, HD), BF16),
            vmem((ROWS, HD), BF16),
            vmem((NCHUNK, 2, 4, 512, HD), BF16),
            vmem((ROWS, GROUP * HD), BF16),
            vmem((TILES, HD, 256), BF16),
            vmem((TILES, 144, 256), F32),
            vmem((TILES, 8, 256), F32),
            vmem((2, 2048, 256), F32),
            vmem((2, 8, 256), F32),
            vmem((ROWS, GROUP * HD), BF16),
            pltpu.SMEM((64,), F32),
            vmem((HD, 128), BF16),
            vmem((2048, 128), F32),
            vmem((144, 128), F32),
            vmem((8, 128), F32),
            vmem((1024, 256), BF16),
            vmem((16, 1024), BF16),
            vmem((16, 1024), BF16),
            vmem((8, 4, 16, 512), BF16),
            vmem((8, 4, 16, 512), BF16),
            vmem((16, 512), BF16),
            vmem((16, 512), BF16),
            vmem((512, 256), F32),
            vmem((512, 256), BF16),
            vmem((4, 128, 256), BF16),
            vmem((4, 8, 128), F32),
            vmem((4, 8, 128), F32),
            vmem((8, 8, 128), F32),
            vmem((4, 8, 128), F32),
            vmem((8, 8, 128), F32),
            dma((3,)), dma((3,)), dma((3,)), dma((8,)), dma((8,)), dma((32,)), dma((32,)),
            dma((NCHUNK,)), dma((NCHUNK,)),
            dma, dma, dma((12,)), dma((12,)), dma((11,)), dma((11,)),
            dma((4,)), dma((4,)), dma((4,)), dma((4,)),
            dma((8,)), dma((8,)), dma((4,)), dma((4,)), dma((8,)), dma((8,)),
        ],
        compiler_params=pltpu.CompilerParams(
            collective_id=0, has_side_effects=True, vmem_limit_bytes=60 * 2**20
        ),
        name="trace_scores",
    )(queries, keys, values, w_in, w_out.T, step_pos.reshape(1, 256), step_attr.reshape(1, 256))
    return attended, logits.T


def solution(mesh):
    in_specs = (
        P("ctx", "head"),
        P("ctx", "head"),
        P("ctx", "head"),
        P("head", "ctx"),
        P("ctx", None),
        P(),
        P(),
    )
    out_specs = (P("ctx", "head"), P())
    return jax.shard_map(body, mesh=mesh, in_specs=in_specs, out_specs=out_specs, check_vma=False)
```
